32 devices in a mesh: grp: 16 (over z, y, x), in: 2 (over core).
Axes of the slice: x: 2, y: 2, z: 4, core: 2. Of those that a mesh axis runs over, the one named last changes fastest.
Arguments:
- inputs: bfloat16 [2, 16, 384, 2048], P(None, 'grp', 'in'), may hold values from -6 to 6
- cotangent: bfloat16 [2, 16, 384, 2048], P(None, 'grp', 'in'), may hold values from -6 to 6
- lengths: int32 [2, 16], P(None, 'grp'), may hold values from 153 to 384, as said below
- w_query: bfloat16 [2048, 2048], P(('grp', 'in')), may hold values from -0.125 to 0.125
- w_key: bfloat16 [2048, 2048], P(('grp', 'in')), may hold values from -0.125 to 0.125
- w_value: bfloat16 [2048, 2048], P(('grp', 'in')), may hold values from -0.125 to 0.125
- w_out: bfloat16 [2048, 2048], P(('grp', 'in')), may hold values from -0.5 to 0.5
- w_gate: bfloat16 [2048, 5632], P(('grp', 'in')), may hold values from -0.125 to 0.125
- w_up: bfloat16 [2048, 5632], P(('grp', 'in')), may hold values from -0.125 to 0.125
- w_down: bfloat16 [5632, 2048], P(('grp', 'in')), may hold values from -0.15625 to 0.15625
- norm_attn: bfloat16 [2048], P(('grp', 'in')), may hold values from 0.5 to 1.5
- norm_head: bfloat16 [2048], P(('grp', 'in')), may hold values from 0.5 to 1.5
- norm_ffn: bfloat16 [2048], P(('grp', 'in')), may hold values from 0.5 to 1.5
- lambda_params: bfloat16 [512], P(('grp', 'in')), may hold values from -0.099609375 to 0.099609375
Outputs:
- output: bfloat16 [2, 16, 384, 2048], P(None, 'grp', 'in')
- input_grad: bfloat16 [2, 16, 384, 2048], P(None, 'grp', 'in')
- grad_w_query: float32 [2048, 2048], P(('grp', 'in'))
- grad_w_key: float32 [2048, 2048], P(('grp', 'in'))
- grad_w_value: float32 [2048, 2048], P(('grp', 'in'))
- grad_w_out: float32 [2048, 2048], P(('grp', 'in'))
- grad_w_gate: float32 [2048, 5632], P(('grp', 'in'))
- grad_w_up: float32 [2048, 5632], P(('grp', 'in'))
- grad_w_down: float32 [5632, 2048], P(('grp', 'in'))
- grad_norm_attn: float32 [2048], P(('grp', 'in'))
- grad_norm_head: float32 [2048], P(('grp', 'in'))
- grad_norm_ffn: float32 [2048], P(('grp', 'in'))
- grad_lambda: float32 [512], P(('grp', 'in'))
The draws below stay inside these ranges and needn't reach their ends.
Inputs may be any that keep to these rules, and one draw needn't show every extreme that they name: Every slot index s has lengths[m, s] = 384 for at least one micro-batch m.
All inputs are finite; a program needn't handle non-finite values.
Results may differ from the reference program's by a relative error of at most 0.018.
The reference program's roundings to bfloat16 on the way count: a program that leaves them out, or rounds other values in their place, can miss the bound.
Values may be sent and summed in bfloat16 or wider, within the bound.
No kernel may reach another device: no remote copies, remote signals or barrier semaphores. Data moves between devices by JAX's collectives and lax.ppermute only.
A program may use at most 448 MiB of HBM per device.

```python
import math
import jax
import jax.numpy as jnp
from jax import lax

D = 2048
H = 8
DH = 128
FF = 5632
L = 384
MB = 2
LMIN = 153
SLOTS = 16


def draw_lengths(key, part):
    base_len = jax.random.randint(jax.random.fold_in(key, 11), (MB, SLOTS), LMIN, L + 1)
    chosen = jax.random.randint(jax.random.fold_in(key, 12), (SLOTS,), 0, MB)
    full_row = jnp.arange(MB)[:, None] == chosen[None, :]
    return jnp.where(full_row, L, base_len).astype(jnp.int32)


def with_spikes(result, own_key, source, target, blocks, factor):
    def block_of(dim):
        return (jnp.arange(result.shape[dim]) // (result.shape[dim] // blocks)).reshape((-1,) + (1,) * (result.ndim - 1 - dim))

    near = jax.random.permutation(own_key, blocks)[block_of(target)]
    second = (block_of(target) + blocks // 2) % blocks
    return jnp.where((block_of(source) == near) | (block_of(source) == second), factor * result, result)


def block_levels(key, shape, shards, least, largest):
    loudness = 1.0
    for dim, shards_of in shards:
        heights = jax.random.uniform(jax.random.fold_in(jax.random.fold_in(key, 6), dim), (shards_of,), jnp.float32, least / len(shards), largest / len(shards))
        loudness = loudness * jnp.repeat(jnp.exp(heights), shape[dim] // shards_of).reshape((-1,) + (1,) * (len(shape) - 1 - dim))
    return loudness


def scatter_about(rng, extent, spread, reach, cuts=(), held_as=jnp.bfloat16):
    values = spread * jax.random.normal(rng, extent, jnp.float32)
    if cuts:
        values = values * block_levels(rng, extent, cuts, -0.22, 0.18)
    return jnp.clip(values, -reach, reach).astype(held_as)


def gaussian_with(stream_key, extent, scale, bound, shards, heavy, held_as=jnp.bfloat16):
    array = scale * jax.random.normal(stream_key, extent, jnp.float32)
    if shards:
        array = array * block_levels(stream_key, extent, shards, -0.22, 0.18)
    return jnp.clip(with_spikes(array, jax.random.fold_in(stream_key, 3), *heavy), -bound, bound).astype(held_as)


def setup_inputs(seed: int = 0) -> dict:
    streams_of = jax.random.split(jax.random.key(seed), 15)
    return {
        "inputs": gaussian_with(streams_of[0], (MB, SLOTS, L, D), 1.0, 6.0, ((1, 16), (2, 2)), (1, 3, 16, 2.0)),
        "cotangent": scatter_about(streams_of[1], (MB, SLOTS, L, D), 1.0, 6.0, ((1, 16), (2, 2))),
        "lengths": draw_lengths(jax.random.fold_in(streams_of[14], 71), 0),
        "w_query": scatter_about(streams_of[3], (D, D), D ** -0.5, 0.125, ((0, 32),)),
        "w_key": scatter_about(streams_of[4], (D, D), D ** -0.5, 0.125, ((0, 32),)),
        "w_value": scatter_about(streams_of[5], (D, D), D ** -0.5, 0.125, ((0, 32),)),
        "w_out": scatter_about(streams_of[6], (D, D), (D // 16) ** -0.5, 0.5, ((0, 32),)),
        "w_gate": scatter_about(streams_of[7], (D, FF), D ** -0.5, 0.125, ((0, 32),)),
        "w_up": scatter_about(streams_of[8], (D, FF), D ** -0.5, 0.125, ((0, 32),)),
        "w_down": scatter_about(streams_of[9], (FF, D), (FF // 4) ** -0.5, 0.15625, ((0, 32),)),
        "norm_attn": jnp.clip(1.0 + 0.1 * jax.random.normal(streams_of[10], (D,), jnp.float32), 0.5, 1.5).astype(jnp.bfloat16),
        "norm_head": jnp.clip(1.0 + 0.1 * jax.random.normal(streams_of[11], (D,), jnp.float32), 0.5, 1.5).astype(jnp.bfloat16),
        "norm_ffn": jnp.clip(1.0 + 0.1 * jax.random.normal(streams_of[12], (D,), jnp.float32), 0.5, 1.5).astype(jnp.bfloat16),
        "lambda_params": scatter_about(streams_of[13], (4 * DH,), 0.04, 0.099609375, ((0, 32),)),
    }


epsilon = 1e-05
lambda_init = 0.8 - 0.6 * math.exp(-3.3)
rope_base = 10000.0
highest = lax.Precision.HIGHEST

@jax.custom_vjp
def low(v):
    return lax.optimization_barrier(v.astype(jnp.bfloat16)).astype(jnp.float32)

@jax.custom_vjp
def low_back(v):
    return v

def low_keep(v):
    return (low(v), None)

def low_pass(kept, grad):
    return (grad,)

def back_keep(v):
    return (v, None)

def back_low(kept, grad):
    return (low(grad),)
low.defvjp(low_keep, low_pass)
low_back.defvjp(back_keep, back_low)

def matmul(left, right):
    return jnp.dot(left, right, precision=highest, preferred_element_type=jnp.float32)

def rms_scale(values, gain):
    return values * lax.rsqrt(lax.optimization_barrier(jnp.mean(values * values, axis=-1, keepdims=True)) + epsilon) * gain

def rope_tables(positions, half_width):
    frequency = rope_base ** (-jnp.arange(half_width, dtype=jnp.float32) / half_width)
    angles = positions.astype(jnp.float32)[:, None] * frequency[None, :]
    return (jnp.cos(angles)[:, None, None, :], jnp.sin(angles)[:, None, None, :])

def rotate(values, cos_table, sin_table, direction):
    half_width = values.shape[-1] // 2
    first_half = values[..., :half_width]
    second_half = values[..., half_width:]
    return jnp.concatenate([first_half * cos_table - direction * second_half * sin_table, second_half * cos_table + direction * first_half * sin_table], axis=-1)

def lambda_value(lambda_params):
    lambda_parts = lambda_params.reshape(4, DH)
    return jnp.exp(jnp.sum(lambda_parts[0] * lambda_parts[1])) - jnp.exp(jnp.sum(lambda_parts[2] * lambda_parts[3])) + lambda_init

def sequence_forward(params, seq_in, length):
    w_query, w_key, w_value, w_out, w_gate, w_up, w_down, norm_attn, norm_head, norm_ffn, lambda_params = params
    rows_count = seq_in.shape[0]
    score_scale = 1.0 / math.sqrt(DH)
    positions = jnp.arange(rows_count, dtype=jnp.int32)
    cos_table, sin_table = rope_tables(positions, DH // 2)
    normed_one = low(rms_scale(seq_in, norm_attn))
    query_raw = low_back(matmul(normed_one, w_query))
    key_raw = low_back(matmul(normed_one, w_key))
    value_low = low(low_back(matmul(normed_one, w_value)))
    query_rot = low(rotate(query_raw.reshape(rows_count, H, 2, DH), cos_table, sin_table, 1.0))
    key_rot = low(rotate(key_raw.reshape(rows_count, H, 2, DH), cos_table, sin_table, 1.0))
    scores = low_back(jnp.einsum('qhmd,khmd->hmqk', query_rot, key_rot, precision=highest) * score_scale)
    allowed = (positions[None, :] <= positions[:, None]) & (positions[None, :] < length)
    masked = jnp.where(allowed, scores, -1e+30)
    top_score = lax.optimization_barrier(jnp.max(masked, axis=-1, keepdims=True))
    exp_terms = jnp.exp(masked - top_score)
    probs_all = exp_terms / lax.optimization_barrier(jnp.sum(exp_terms, axis=-1, keepdims=True))
    combined = low(probs_all[:, 0] - lambda_value(lambda_params) * probs_all[:, 1])
    attended = low_back(jnp.einsum('hqk,khe->qhe', combined, value_low.reshape(rows_count, H, 2 * DH), precision=highest))
    head_gain = norm_head.reshape(H, 2 * DH) * (1.0 - lambda_init)
    headed = low(rms_scale(attended, head_gain)).reshape(rows_count, H * 2 * DH)
    residual = seq_in + low_back(matmul(headed, w_out))
    normed_two = low(rms_scale(residual, norm_ffn))
    gate_val = low_back(matmul(normed_two, w_gate))
    up_val = low_back(matmul(normed_two, w_up))
    hidden = low(jax.nn.silu(gate_val) * up_val)
    block_out = residual + low_back(matmul(hidden, w_down))
    return jnp.where((positions < length)[:, None], block_out, 0.0)

def reference(inputs, cotangent, lengths, w_query, w_key, w_value, w_out, w_gate, w_up, w_down, norm_attn, norm_head, norm_ffn, lambda_params):
    params = tuple((weight_arr.astype(jnp.float32) for weight_arr in (w_query, w_key, w_value, w_out, w_gate, w_up, w_down, norm_attn, norm_head, norm_ffn, lambda_params)))
    seq_inputs = inputs.astype(jnp.float32).reshape(MB * SLOTS, L, D)
    seq_grads = cotangent.astype(jnp.float32).reshape(MB * SLOTS, L, D)
    seq_lengths = lengths.reshape(MB * SLOTS).astype(jnp.int32)

    def one_sequence(totals, scan_item):
        seq_in, seq_ct, length = scan_item

        def local_fn(weights, block_in):
            return sequence_forward(weights, block_in, length)
        block_out, pull_back = jax.vjp(local_fn, params, seq_in)
        grad_params, grad_in = pull_back(seq_ct)
        totals = jax.tree.map(jnp.add, totals, grad_params)
        return (totals, (block_out.astype(jnp.bfloat16), grad_in.astype(jnp.bfloat16)))
    zero_grads = jax.tree.map(jnp.zeros_like, params)
    totals, (outputs, input_grads) = lax.scan(one_sequence, zero_grads, (seq_inputs, seq_grads, seq_lengths))
    return (outputs.reshape(MB, SLOTS, L, D), input_grads.reshape(MB, SLOTS, L, D), totals[0], totals[1], totals[2], totals[3], totals[4], totals[5], totals[6], totals[7], totals[8], totals[9], totals[10])
```

```python
import functools
import math

import jax
import jax.numpy as jnp
from jax import lax
from jax.experimental import pallas as pl
from jax.experimental.pallas import tpu as pltpu
from jax.sharding import Mesh
from jax.sharding import PartitionSpec as P

H = 8
DH = 128
TEAM = ("y", "x", "c")
ROWS = ("c", "y", "x")
EVERY = ("z", "y", "x", "c")

epsilon = 1e-05
lambda_init = 0.8 - 0.6 * math.exp(-3.3)
rope_base = 10000.0
score_scale = 1.0 / math.sqrt(DH)
bf16 = jnp.bfloat16
f32 = jnp.float32


def product(left, right):
    return jnp.dot(left, right, preferred_element_type=f32)


def contract_rows(left, right):
    return lax.dot_general(left, right, (((0,), (0,)), ((), ())), preferred_element_type=f32)


def against(left, right):
    return lax.dot_general(left, right, (((1,), (1,)), ((), ())), preferred_element_type=f32)


def inverse_rms(values):
    return lax.rsqrt(jnp.mean(values * values, axis=-1, keepdims=True) + epsilon)


def norm_back(grad_unit, unit_vals, inverse):
    return inverse * (
        grad_unit - unit_vals * jnp.mean(grad_unit * unit_vals, axis=-1, keepdims=True)
    )


def turn(values, cos_table, sin_table):
    return values * cos_table + pltpu.roll(values, DH // 2, 1) * sin_table


def softmax_block(query, key, allowed):
    scores = jnp.where(allowed, against(query, key) * score_scale, -1e30)
    terms = jnp.exp(scores - jnp.max(scores, axis=-1, keepdims=True))
    return terms / jnp.sum(terms, axis=-1, keepdims=True)


def allowed_block(start, rows, keys, length):
    row = start + lax.broadcasted_iota(jnp.int32, (rows, keys), 0)
    col = lax.broadcasted_iota(jnp.int32, (rows, keys), 1)
    return (col <= row) & (col < length)


def attend_kernel(len_ref, lam_ref, raw_ref, cos_ref, sin_ref, gain_ref, rot_ref, headed_ref):
    length = len_ref[pl.program_id(0), pl.program_id(1)]
    lam = lam_ref[0]
    halves, rows = raw_ref.shape[0], raw_ref.shape[3]
    total = halves * rows
    raw = raw_ref[:, 0, 0].reshape(total, 6 * DH)
    cos_table, sin_table = cos_ref[...], sin_ref[...]
    turned = [
        turn(raw[:, part * DH : (part + 1) * DH], cos_table, sin_table).astype(bf16)
        for part in range(4)
    ]
    value = raw[:, 4 * DH :].astype(bf16)
    rot_ref[:, 0, 0] = jnp.concatenate(turned + [value], axis=1).reshape(halves, rows, 6 * DH)
    gain = gain_ref[...]
    step = 128
    parts = []
    for start in range(0, total, step):
        keys = start + step
        mask = allowed_block(start, step, keys, length)
        first = softmax_block(turned[0][start:keys], turned[2][:keys], mask)
        second = softmax_block(turned[1][start:keys], turned[3][:keys], mask)
        combined = (first - lam * second).astype(bf16)
        attended = product(combined, value[:keys])
        parts.append((attended * inverse_rms(attended) * gain).astype(bf16))
    headed_ref[:, 0, 0] = jnp.concatenate(parts, axis=0).reshape(halves, rows, 2 * DH)


def attend_back_kernel(
    len_ref, lam_ref, rot_ref, grad_ref, cos_ref, sin_ref, gain_ref,
    out_ref, head_ref, lam_out_ref, grad_key, grad_value,
):
    first_step = (pl.program_id(0) == 0) & (pl.program_id(1) == 0)

    @pl.when(first_step)
    def _():
        head_ref[...] = jnp.zeros_like(head_ref)
        lam_out_ref[...] = jnp.zeros_like(lam_out_ref)

    length = len_ref[pl.program_id(0), pl.program_id(1)]
    lam = lam_ref[0]
    halves, rows = rot_ref.shape[0], rot_ref.shape[3]
    total = halves * rows
    rot = rot_ref[:, 0, 0].reshape(total, 6 * DH)
    grad_headed = grad_ref[:, 0, 0].reshape(total, 2 * DH).astype(f32)
    cos_table, sin_table = cos_ref[...], sin_ref[...]
    query = [rot[:, :DH], rot[:, DH : 2 * DH]]
    key = [rot[:, 2 * DH : 3 * DH], rot[:, 3 * DH : 4 * DH]]
    value = rot[:, 4 * DH :]
    gain = gain_ref[...]
    step = 128
    grad_query = [[], []]
    for start in reversed(range(0, total, step)):
        keys = start + step
        mask = allowed_block(start, step, keys, length)
        first = softmax_block(query[0][start:keys], key[0][:keys], mask)
        second = softmax_block(query[1][start:keys], key[1][:keys], mask)
        combined = (first - lam * second).astype(bf16)
        attended = product(combined, value[:keys])
        inverse = inverse_rms(attended)
        unit = attended * inverse
        grad_head = grad_headed[start:keys]
        head_ref[...] += jnp.sum(grad_head * unit, axis=0, keepdims=True)
        grad_attended = norm_back(grad_head * gain, unit, inverse).astype(bf16)
        grad_comb = against(grad_attended, value[:keys])
        value_part = contract_rows(combined, grad_attended)
        inner = [
            jnp.sum(grad_comb * first, axis=-1, keepdims=True),
            jnp.sum(grad_comb * second, axis=-1, keepdims=True),
        ]
        lam_out_ref[...] -= jnp.sum(inner[1], axis=0, keepdims=True)
        grad_scores = [
            (first * (grad_comb - inner[0])).astype(bf16),
            (-lam * second * (grad_comb - inner[1])).astype(bf16),
        ]
        if keys == total:
            grad_value[...] = value_part
        else:
            grad_value[:keys] += value_part
        for k in range(2):
            key_part = contract_rows(grad_scores[k], query[k][start:keys])
            cols = slice(k * DH, (k + 1) * DH)
            if keys == total:
                grad_key[:, cols] = key_part
            else:
                grad_key[:keys, cols] += key_part
            grad_query[k].append(product(grad_scores[k], key[k][:keys]) * score_scale)
    turned = [
        turn(jnp.concatenate(grad_query[k][::-1], axis=0), cos_table, sin_table).astype(bf16)
        for k in range(2)
    ] + [
        turn(grad_key[:, k * DH : (k + 1) * DH] * score_scale, cos_table, sin_table).astype(bf16)
        for k in range(2)
    ]
    out_ref[:, 0, 0] = jnp.concatenate(
        turned + [grad_value[...].astype(bf16)], axis=1
    ).reshape(halves, rows, 6 * DH)


def row_spec(halves, rows, cols):
    return pl.BlockSpec((halves, 1, 1, rows, cols), lambda j, m: (0, j, m, 0, 0))


def whole_spec(shape):
    return pl.BlockSpec(shape, lambda j, m: (0,) * len(shape))


def attend(lengths, lam, raw, cos_table, sin_table, gain, dims):
    halves, slots, batches, rows = dims
    smem = pl.BlockSpec(memory_space=pltpu.SMEM)
    rot, headed = pl.pallas_call(
        attend_kernel,
        grid=(slots, batches),
        in_specs=[
            smem, smem, row_spec(halves, rows, 6 * DH),
            whole_spec(cos_table.shape), whole_spec(sin_table.shape), whole_spec(gain.shape),
        ],
        out_specs=[row_spec(halves, rows, 6 * DH), row_spec(halves, rows, 2 * DH)],
        out_shape=[
            jax.ShapeDtypeStruct(dims + (6 * DH,), bf16),
            jax.ShapeDtypeStruct(dims + (2 * DH,), bf16),
        ],
        compiler_params=pltpu.CompilerParams(vmem_limit_bytes=48 * 1024 * 1024),
    )(lengths, lam, raw.reshape(dims + (6 * DH,)), cos_table, sin_table, gain)
    return rot, headed


def attend_back(lengths, lam, rot, grad_headed, cos_table, sin_table, gain, dims):
    halves, slots, batches, rows = dims
    smem = pl.BlockSpec(memory_space=pltpu.SMEM)
    return pl.pallas_call(
        attend_back_kernel,
        grid=(slots, batches),
        in_specs=[
            smem, smem, row_spec(halves, rows, 6 * DH), row_spec(halves, rows, 2 * DH),
            whole_spec(cos_table.shape), whole_spec(sin_table.shape), whole_spec(gain.shape),
        ],
        out_specs=[
            row_spec(halves, rows, 6 * DH), whole_spec((1, 2 * DH)), whole_spec((1, 128)),
        ],
        out_shape=[
            jax.ShapeDtypeStruct(dims + (6 * DH,), bf16),
            jax.ShapeDtypeStruct((1, 2 * DH), f32),
            jax.ShapeDtypeStruct((1, 128), f32),
        ],
        scratch_shapes=[
            pltpu.VMEM((halves * rows, 2 * DH), f32),
            pltpu.VMEM((halves * rows, 2 * DH), f32),
        ],
        compiler_params=pltpu.CompilerParams(vmem_limit_bytes=48 * 1024 * 1024),
    )(lengths, lam, rot, grad_headed.reshape(dims + (2 * DH,)), cos_table, sin_table, gain)


def shift(depth, step):
    return [(i, (i + step) % depth) for i in range(depth)]


def after(value, *others):
    return lax.optimization_barrier((value, *others))[0]


def permute(value, depth, step):
    return lax.ppermute(value, "z", shift(depth, step))


class Gather:
    def __init__(self, block, depth, hold=None):
        self.block, self.depth = block, depth
        self.near = [(block, block)]
        for _ in range((depth - 1) // 2):
            above, below = self.near[-1]
            pair = (permute(above, depth, -1), permute(below, depth, 1))
            self.near.append(pair if hold is None else hold(pair))
        self.far = None
        if depth % 2 == 0:
            above, below = self.near[-1]
            half = block.shape[0] // 2
            self.far = (permute(above[:half], depth, -1), permute(below[half:], depth, 1))

    def joined(self, axis, *others):
        near, far = self.near[1:], self.far
        if others:
            near, far, _ = lax.optimization_barrier((near, far, others))
        middle = [] if far is None else [jnp.concatenate(far, axis=0)]
        above = [pair[0] for pair in near]
        below = [pair[1] for pair in near[::-1]]
        return jnp.concatenate([self.block] + above + middle + below, axis=axis)

    def first(self):
        return self.near[-1]

    def last(self):
        return self.near[-1] if self.far is None else self.far


class Scatter:
    def __init__(self, blocks):
        depth = len(blocks)
        half = blocks[0].shape[0] // 2
        self.pairs = [
            [(blocks[k][:half], blocks[-k % depth][half:]) for k in range(depth // 2 + 1)],
            [(blocks[k][half:], blocks[-k % depth][:half]) for k in range((depth - 1) // 2 + 1)],
        ]
        self.depth = depth
        self.first = self.move(self.pairs[0][-1]) if depth > 1 else None

    def move(self, pair):
        return (permute(pair[0], self.depth, 1), permute(pair[1], self.depth, -1))

    def chain(self, pairs, moved):
        for pair in pairs[-2:0:-1]:
            moved = self.move(
                tuple((a.astype(f32) + b.astype(f32)).astype(bf16) for a, b in zip(pair, moved))
            )
        return moved

    def plain(self):
        pairs = self.pairs[1]
        self.second = self.chain(pairs, self.move(pairs[-1])) if len(pairs) > 1 else None
        return self.second

    def added(self, *others):
        pairs = self.pairs[0]
        self.third = self.chain(pairs, after(self.first, *others)) if self.depth > 1 else None
        return self.third

    def total(self, *others):
        (top, _), (bottom, _) = self.pairs[0][0], self.pairs[1][0]
        bottom = self.pairs[0][0][1]
        top, bottom = top.astype(f32), bottom.astype(f32)
        third, second, _ = lax.optimization_barrier((self.third, self.second, others))
        for pair, swap in ((third, False), (second, True)):
            if pair is not None:
                up, down = pair[::-1] if swap else pair
                top, bottom = top + up.astype(f32), bottom + down.astype(f32)
        return jnp.concatenate([top, bottom], axis=0)


def turn_blocks(values, depth, axis, forth=True):
    size = values.shape[axis]
    here = lax.axis_index("z")
    start = (here if forth else (depth - here) % depth) * (size // depth)
    return lax.dynamic_slice_in_dim(
        jnp.concatenate([values, values], axis=axis), start, size, axis
    )


def gather_rows(block):
    return lax.all_gather(block, ROWS, axis=0, tiled=True)


def exchange(values, split, joined, order=ROWS):
    return lax.all_to_all(values, order, split_axis=split, concat_axis=joined, tiled=True)


def split_cores(values, axis=0):
    count = values.shape[axis] // 2
    mine = lax.axis_index("c")
    return [
        lax.dynamic_slice_in_dim(values, core * count, count, axis) for core in (1 - mine, mine)
    ]


def across(values):
    values = values.astype(bf16)
    return values, lax.ppermute(values, "c", [(0, 1), (1, 0)])


def over_cores(compute, theirs, mine):
    return compute(mine) + across(compute(theirs))[1].astype(f32)


def over_chips(total):
    return lax.psum_scatter(total.astype(bf16), ("y", "x"), scatter_dimension=0, tiled=True)


def body(
    inputs, cotangent, lengths, w_query, w_key, w_value, w_out, w_gate, w_up, w_down,
    norm_attn, norm_head, norm_ffn, lambda_params, *, depth,
):
    batches, _, rows, width = inputs.shape
    team = H
    chips = team // 2
    shard = w_query.shape[0]
    hidden_shard = w_down.shape[0]
    own_rows = batches * rows
    dims = (2, chips, batches, rows)
    total_rows = 2 * rows
    places = depth * team
    units = depth * hidden_shard
    turned = functools.partial(turn_blocks, depth=depth)

    def natural(blocks):
        shape = blocks.shape
        blocks = blocks.reshape((2, chips, shape[0] // team) + shape[1:])
        return jnp.swapaxes(blocks, 0, 1).reshape(shape)

    def by_core(blocks):
        shape = blocks.shape
        blocks = blocks.reshape((chips, 2, shape[0] // team) + shape[1:])
        return jnp.swapaxes(blocks, 0, 1).reshape(shape)

    x_own = inputs.reshape(own_rows, width)
    x_all = gather_rows(turned(x_own, axis=1))

    qkv = jnp.concatenate(
        [w.reshape(shard, H, 2 * DH) for w in (w_query, w_key, w_value)], axis=2
    )
    qkv = exchange(qkv.transpose(1, 0, 2).reshape(H * shard, 6 * DH), 0, 0)

    small = jnp.concatenate(
        [
            norm_attn.astype(f32), norm_head.astype(f32), norm_ffn.astype(f32),
            lambda_params.astype(f32), lengths[:, 0].astype(f32),
        ]
    )[None]
    small = lax.all_gather(after(small, qkv), TEAM, axis=0, tiled=True)
    length_all = small[:, -batches:].reshape(chips, 2, batches)[:, 0].astype(jnp.int32)
    far_small = [permute(small, depth, -k) for k in range(1, depth)]
    qkv_ring = Gather(natural(qkv), depth, lambda near: after(near, far_small))
    small = jnp.concatenate([small] + far_small, axis=0).reshape(depth, team, -1)
    small = turned(small, axis=0, forth=False)
    qkv_near = qkv_ring.first()
    out_w = lax.all_gather(w_out, EVERY, axis=0, tiled=True)

    def by_units(w):
        w = w.reshape(shard, depth, team, hidden_shard).transpose(2, 0, 1, 3)
        return w.reshape(team * shard, units)

    gate_up = jnp.concatenate([by_units(w_gate), by_units(w_up)], axis=1)
    def to_units(grad):
        grad = grad.reshape(team, shard, depth, hidden_shard).transpose(1, 2, 0, 3)
        return grad.reshape(shard, places * hidden_shard)

    n_lam = lambda_params.shape[0]
    gain_attn = small[:, :, :shard].reshape(1, width)
    gain_head = small[:, :, shard : 2 * shard].reshape(H, 2 * DH)
    gain_ffn = small[:, :, 2 * shard : 3 * shard].reshape(1, width)
    lam_parts = small[:, :, 3 * shard : 3 * shard + n_lam].reshape(4, DH)
    first_exp = jnp.exp(jnp.sum(lam_parts[0] * lam_parts[1]))
    second_exp = jnp.exp(jnp.sum(lam_parts[2] * lam_parts[3]))
    lam = (first_exp - second_exp + lambda_init)[None]
    head = lax.axis_index(ROWS)
    gain_mine = lax.dynamic_index_in_dim(gain_head, head, 0) * (1.0 - lambda_init)

    frequency = rope_base ** (-jnp.arange(DH // 2, dtype=f32) / (DH // 2))
    angles = jnp.arange(total_rows, dtype=f32)[:, None] * frequency[None, :]
    cos_table = jnp.concatenate([jnp.cos(angles)] * 2, axis=1)
    sine = jnp.sin(angles)
    sin_table = jnp.concatenate([-sine, sine], axis=1)

    x_float = after(x_all, *qkv_near).astype(f32)
    inverse_all = inverse_rms(x_float)
    normed_one = (x_float * inverse_all * turned(gain_attn, axis=1)).astype(bf16)
    qkv_w = qkv_ring.joined(0, normed_one)
    gate_up = exchange(after(gate_up, normed_one), 0, 0, TEAM).T
    gate_up_ring = Gather(gate_up, depth)
    gate_up_w = gate_up_ring.joined(1)
    down_ring = Gather(after(w_down, *gate_up_ring.first()), depth)
    raw = product(normed_one, qkv_w)
    rot, headed = attend(length_all, lam, after(raw, gate_up), cos_table, sin_table, gain_mine, dims)
    headed_own = exchange(headed.reshape(team * own_rows, 2 * DH), 0, 1)
    headed_own = after(headed_own, *gate_up_ring.first())

    x_own = x_own.astype(f32)
    residual = x_own + product(headed_own, out_w)
    inverse_two = inverse_rms(residual)
    unit_two = residual * inverse_two
    normed_two = gather_rows(turned((unit_two * gain_ffn).astype(bf16), axis=1))

    positions = lax.axis_index("c") * rows + jnp.arange(rows, dtype=jnp.int32)
    valid = (positions[None, :] < lengths).reshape(own_rows, 1)
    grad_own = jnp.where(valid, cotangent.reshape(own_rows, width), 0)
    grad_all = gather_rows(grad_own)

    gate_up_val = against(gate_up_w, normed_two)
    gate_val, up_val = gate_up_val[:units], gate_up_val[units:]
    down_w = turned(down_ring.joined(0, gate_up_val), axis=0, forth=False)
    sigmoid_gate = jax.nn.sigmoid(gate_val)
    activation = gate_val * sigmoid_gate
    hidden = (activation * up_val).astype(bf16)

    def over_units(weight):
        return lambda values: contract_rows(values, weight)

    out_rows = over_cores(over_units(down_w), *split_cores(hidden, 1)).astype(bf16)
    grad_hidden = against(down_w, after(grad_all, out_rows))
    grad_gate = grad_hidden * up_val * sigmoid_gate * (1.0 + gate_val * (1.0 - sigmoid_gate))
    grad_up = grad_hidden * activation
    grad_gate_up = jnp.concatenate([grad_gate.astype(bf16), grad_up.astype(bf16)], axis=0)

    out_rows = over_chips(out_rows)
    theirs, mine = split_cores(grad_gate_up, 1)
    sent = across(over_units(gate_up_w)(theirs))
    grad_w_down = product(hidden, after(grad_all, sent[0])).astype(bf16)
    down_blocks = grad_w_down.reshape(depth, hidden_shard, width)
    down_back = Scatter(
        [
            lax.dynamic_index_in_dim(down_blocks, (lax.axis_index("z") + k) % depth, 0, False)
            for k in range(depth)
        ]
    )
    grad_two = over_units(gate_up_w)(after(mine, grad_w_down))
    grad_two = (grad_two + sent[1].astype(f32)).astype(bf16)
    down_back.plain()
    grad_w_gate_up = product(after(grad_gate_up, grad_two), normed_two).astype(bf16)
    down_back.added(*down_back.second, grad_w_gate_up)
    gate_up_back = Scatter(jnp.split(grad_w_gate_up, depth, axis=1))
    gate_up_back.plain()
    gate_up_back.added()
    grad_w_down = down_back.total()
    grad_two = after(over_chips(after(grad_two, out_rows)), grad_w_down, *gate_up_back.first)
    grad_two = turned(grad_two, axis=1, forth=False).astype(f32)

    grad_norm_ffn = jnp.sum(grad_two * unit_two, axis=0)
    grad_resid = grad_own.astype(f32) + norm_back(grad_two * gain_ffn, unit_two, inverse_two)
    grad_branch = grad_resid.astype(bf16)
    grad_headed = exchange(against(grad_branch, out_w).astype(bf16), 1, 0)
    headed_cores = headed_own.reshape(own_rows, depth, chips, 2, shard).transpose(0, 3, 2, 1, 4)
    headed_cores = turned(headed_cores, axis=3).reshape(own_rows, width)
    grad_w_out = over_cores(lambda v: contract_rows(v, grad_branch), *split_cores(headed_cores, 1))
    grad_w_out = grad_w_out.astype(bf16)
    grad_headed = after(grad_headed, grad_w_out, *gate_up_back.second)
    grad_w_out = over_chips(grad_w_out)
    grad_raw, grad_head, grad_lam = attend_back(
        length_all, lam, rot, grad_headed, cos_table, -sin_table, gain_mine, dims
    )
    grad_raw = grad_raw.reshape(team * own_rows, 6 * DH)
    out_rows = after(out_rows, grad_raw)
    output = jnp.where(valid, residual + out_rows.astype(f32), 0.0).astype(bf16)
    theirs, mine = split_cores(grad_raw)
    sent = across(against(theirs, qkv_w))
    grad_qkv = contract_rows(normed_one, after(grad_raw, sent[0], *gate_up_back.third)).astype(bf16)
    qkv_back = Scatter(jnp.split(grad_qkv, depth, axis=0))
    grad_w_gate_up = gate_up_back.total(grad_qkv)
    grad_w_gate_up = exchange(grad_w_gate_up.astype(bf16).T, 0, 0, TEAM).astype(f32)
    grad_one = against(after(mine, grad_qkv), qkv_w) + sent[1].astype(f32)
    unit_mine = split_cores(x_all)[1].astype(f32) * split_cores(inverse_all)[1]
    grad_norm_attn = turned(jnp.sum(grad_one * unit_mine, axis=0), axis=0, forth=False)
    grad_one = over_chips(grad_one)
    grad_w_gate = to_units(grad_w_gate_up[:, :units])
    grad_w_up = to_units(grad_w_gate_up[:, units:])
    qkv_back.plain()
    qkv_back.added(grad_w_gate_up)
    out_back = Scatter(jnp.split(after(grad_w_out, *qkv_back.first), depth, axis=0))
    out_back.plain()
    out_back.added()
    grad_w_out = out_back.total()
    grad_lam = grad_lam[0, 0]
    grad_lambda = jnp.concatenate(
        [
            grad_lam * first_exp * lam_parts[1],
            grad_lam * first_exp * lam_parts[0],
            -grad_lam * second_exp * lam_parts[3],
            -grad_lam * second_exp * lam_parts[2],
        ]
    )
    grad_head = grad_head * (1.0 - lambda_init)
    head_full = lax.dynamic_update_slice(jnp.zeros((H, 2 * DH), f32), grad_head, (head, 0))
    small_grads = jnp.concatenate(
        [
            grad_norm_attn.reshape(places, shard),
            head_full.reshape(places, shard),
            grad_norm_ffn.reshape(places, shard),
            grad_lambda.reshape(places, n_lam),
        ],
        axis=1,
    )
    small_grads = small_grads.reshape(depth, team, -1).swapaxes(0, 1).reshape(places, -1)
    small_grads = exchange(small_grads, 0, 0, TEAM).reshape(team, depth, -1).sum(axis=0)
    small_grads = lax.all_to_all(small_grads, "z", 0, 0, tiled=True).sum(axis=0)

    grad_qkv = exchange(by_core(qkv_back.total(small_grads, grad_w_gate, grad_w_up)).astype(bf16), 0, 0).astype(f32)
    grad_qkv = grad_qkv.reshape(H, shard, 3, 2 * DH).transpose(2, 1, 0, 3)
    grad_qkv = grad_qkv.reshape(3, shard, width)

    inverse_one = inverse_rms(x_own)
    grad_one = after(grad_one, small_grads, grad_w_gate, grad_w_up, grad_w_out)
    grad_one = turned(grad_one, axis=1, forth=False).astype(f32)
    unit_one = x_own * inverse_one
    input_grad = (
        grad_resid + norm_back(grad_one * gain_attn, unit_one, inverse_one)
    ).astype(bf16)

    return (
        output.reshape(inputs.shape),
        input_grad.reshape(inputs.shape),
        grad_qkv[0],
        grad_qkv[1],
        grad_qkv[2],
        grad_w_out,
        grad_w_gate,
        grad_w_up,
        grad_w_down,
        small_grads[:shard],
        small_grads[shard : 2 * shard],
        small_grads[2 * shard : 3 * shard],
        small_grads[3 * shard :],
    )


def solution(mesh):
    cores = mesh.shape["in"]
    depth = mesh.shape["grp"] * cores // H
    split = Mesh(mesh.devices.reshape(depth, 2, H // (2 * cores), cores), EVERY)
    group = ("z", "y", "x")
    data = P(None, group, "c", None)
    matrix = P(EVERY, None)
    vector = P(EVERY)
    return jax.shard_map(
        functools.partial(body, depth=depth),
        mesh=split,
        in_specs=(data, data, P(None, group)) + (matrix,) * 7 + (vector,) * 4,
        out_specs=(data, data) + (matrix,) * 7 + (vector,) * 4,
        check_vma=False,
    )
```

```python
import functools
import math

import jax
import jax.numpy as jnp
from jax import lax
from jax.experimental import pallas as pl
from jax.experimental.pallas import tpu as pltpu
from jax.sharding import Mesh
from jax.sharding import PartitionSpec as P

H = 8
DH = 128
TEAM = ("y", "x", "c")
ROWS = ("c", "y", "x")
EVERY = ("z", "y", "x", "c")

epsilon = 1e-05
lambda_init = 0.8 - 0.6 * math.exp(-3.3)
rope_base = 10000.0
score_scale = 1.0 / math.sqrt(DH)
bf16 = jnp.bfloat16
f32 = jnp.float32


def product(left, right):
    return jnp.dot(left, right, preferred_element_type=f32)


def contract_rows(left, right):
    return lax.dot_general(left, right, (((0,), (0,)), ((), ())), preferred_element_type=f32)


def against(left, right):
    return lax.dot_general(left, right, (((1,), (1,)), ((), ())), preferred_element_type=f32)


def inverse_rms(values):
    return lax.rsqrt(jnp.mean(values * values, axis=-1, keepdims=True) + epsilon)


def norm_back(grad_unit, unit_vals, inverse):
    return inverse * (
        grad_unit - unit_vals * jnp.mean(grad_unit * unit_vals, axis=-1, keepdims=True)
    )


def turn(values, cos_table, sin_table):
    return values * cos_table + pltpu.roll(values, DH // 2, 1) * sin_table


def softmax_block(query, key, allowed):
    scores = jnp.where(allowed, against(query, key) * score_scale, -1e30)
    terms = jnp.exp(scores - jnp.max(scores, axis=-1, keepdims=True))
    return terms / jnp.sum(terms, axis=-1, keepdims=True)


def allowed_block(start, rows, keys, length):
    row = start + lax.broadcasted_iota(jnp.int32, (rows, keys), 0)
    col = lax.broadcasted_iota(jnp.int32, (rows, keys), 1)
    return (col <= row) & (col < length)


def attend_kernel(len_ref, lam_ref, raw_ref, cos_ref, sin_ref, gain_ref, rot_ref, headed_ref):
    length = len_ref[pl.program_id(0), pl.program_id(1)]
    lam = lam_ref[0]
    halves, rows = raw_ref.shape[0], raw_ref.shape[3]
    total = halves * rows
    raw = raw_ref[:, 0, 0].reshape(total, 6 * DH)
    cos_table, sin_table = cos_ref[...], sin_ref[...]
    turned = [
        turn(raw[:, part * DH : (part + 1) * DH], cos_table, sin_table).astype(bf16)
        for part in range(4)
    ]
    value = raw[:, 4 * DH :].astype(bf16)
    rot_ref[:, 0, 0] = jnp.concatenate(turned + [value], axis=1).reshape(halves, rows, 6 * DH)
    gain = gain_ref[...]
    step = 128
    parts = []
    for start in range(0, total, step):
        keys = start + step
        mask = allowed_block(start, step, keys, length)
        first = softmax_block(turned[0][start:keys], turned[2][:keys], mask)
        second = softmax_block(turned[1][start:keys], turned[3][:keys], mask)
        combined = (first - lam * second).astype(bf16)
        attended = product(combined, value[:keys])
        parts.append((attended * inverse_rms(attended) * gain).astype(bf16))
    headed_ref[:, 0, 0] = jnp.concatenate(parts, axis=0).reshape(halves, rows, 2 * DH)


def attend_back_kernel(
    len_ref, lam_ref, rot_ref, grad_ref, cos_ref, sin_ref, gain_ref,
    out_ref, head_ref, lam_out_ref, grad_key, grad_value,
):
    first_step = (pl.program_id(0) == 0) & (pl.program_id(1) == 0)

    @pl.when(first_step)
    def _():
        head_ref[...] = jnp.zeros_like(head_ref)
        lam_out_ref[...] = jnp.zeros_like(lam_out_ref)

    length = len_ref[pl.program_id(0), pl.program_id(1)]
    lam = lam_ref[0]
    halves, rows = rot_ref.shape[0], rot_ref.shape[3]
    total = halves * rows
    rot = rot_ref[:, 0, 0].reshape(total, 6 * DH)
    grad_headed = grad_ref[:, 0, 0].reshape(total, 2 * DH).astype(f32)
    cos_table, sin_table = cos_ref[...], sin_ref[...]
    query = [rot[:, :DH], rot[:, DH : 2 * DH]]
    key = [rot[:, 2 * DH : 3 * DH], rot[:, 3 * DH : 4 * DH]]
    value = rot[:, 4 * DH :]
    gain = gain_ref[...]
    step = 128
    grad_query = [[], []]
    for start in reversed(range(0, total, step)):
        keys = start + step
        mask = allowed_block(start, step, keys, length)
        first = softmax_block(query[0][start:keys], key[0][:keys], mask)
        second = softmax_block(query[1][start:keys], key[1][:keys], mask)
        combined = (first - lam * second).astype(bf16)
        attended = product(combined, value[:keys])
        inverse = inverse_rms(attended)
        unit = attended * inverse
        grad_head = grad_headed[start:keys]
        head_ref[...] += jnp.sum(grad_head * unit, axis=0, keepdims=True)
        grad_attended = norm_back(grad_head * gain, unit, inverse).astype(bf16)
        grad_comb = against(grad_attended, value[:keys])
        value_part = contract_rows(combined, grad_attended)
        inner = [
            jnp.sum(grad_comb * first, axis=-1, keepdims=True),
            jnp.sum(grad_comb * second, axis=-1, keepdims=True),
        ]
        lam_out_ref[...] -= jnp.sum(inner[1], axis=0, keepdims=True)
        grad_scores = [
            (first * (grad_comb - inner[0])).astype(bf16),
            (-lam * second * (grad_comb - inner[1])).astype(bf16),
        ]
        if keys == total:
            grad_value[...] = value_part
        else:
            grad_value[:keys] += value_part
        for k in range(2):
            key_part = contract_rows(grad_scores[k], query[k][start:keys])
            cols = slice(k * DH, (k + 1) * DH)
            if keys == total:
                grad_key[:, cols] = key_part
            else:
                grad_key[:keys, cols] += key_part
            grad_query[k].append(product(grad_scores[k], key[k][:keys]) * score_scale)
    turned = [
        turn(jnp.concatenate(grad_query[k][::-1], axis=0), cos_table, sin_table).astype(bf16)
        for k in range(2)
    ] + [
        turn(grad_key[:, k * DH : (k + 1) * DH] * score_scale, cos_table, sin_table).astype(bf16)
        for k in range(2)
    ]
    out_ref[:, 0, 0] = jnp.concatenate(
        turned + [grad_value[...].astype(bf16)], axis=1
    ).reshape(halves, rows, 6 * DH)


def row_spec(halves, rows, cols):
    return pl.BlockSpec((halves, 1, 1, rows, cols), lambda j, m: (0, j, m, 0, 0))


def whole_spec(shape):
    return pl.BlockSpec(shape, lambda j, m: (0,) * len(shape))


def attend(lengths, lam, raw, cos_table, sin_table, gain, dims):
    halves, slots, batches, rows = dims
    smem = pl.BlockSpec(memory_space=pltpu.SMEM)
    rot, headed = pl.pallas_call(
        attend_kernel,
        grid=(slots, batches),
        in_specs=[
            smem, smem, row_spec(halves, rows, 6 * DH),
            whole_spec(cos_table.shape), whole_spec(sin_table.shape), whole_spec(gain.shape),
        ],
        out_specs=[row_spec(halves, rows, 6 * DH), row_spec(halves, rows, 2 * DH)],
        out_shape=[
            jax.ShapeDtypeStruct(dims + (6 * DH,), bf16),
            jax.ShapeDtypeStruct(dims + (2 * DH,), bf16),
        ],
        compiler_params=pltpu.CompilerParams(vmem_limit_bytes=48 * 1024 * 1024),
        cost_estimate=pl.CostEstimate(flops=1, bytes_accessed=1, transcendentals=0),
    )(lengths, lam, raw.reshape(dims + (6 * DH,)), cos_table, sin_table, gain)
    return rot, headed


def attend_back(lengths, lam, rot, grad_headed, cos_table, sin_table, gain, dims):
    halves, slots, batches, rows = dims
    smem = pl.BlockSpec(memory_space=pltpu.SMEM)
    return pl.pallas_call(
        attend_back_kernel,
        grid=(slots, batches),
        in_specs=[
            smem, smem, row_spec(halves, rows, 6 * DH), row_spec(halves, rows, 2 * DH),
            whole_spec(cos_table.shape), whole_spec(sin_table.shape), whole_spec(gain.shape),
        ],
        out_specs=[
            row_spec(halves, rows, 6 * DH), whole_spec((1, 2 * DH)), whole_spec((1, 128)),
        ],
        out_shape=[
            jax.ShapeDtypeStruct(dims + (6 * DH,), bf16),
            jax.ShapeDtypeStruct((1, 2 * DH), f32),
            jax.ShapeDtypeStruct((1, 128), f32),
        ],
        scratch_shapes=[
            pltpu.VMEM((halves * rows, 2 * DH), f32),
            pltpu.VMEM((halves * rows, 2 * DH), f32),
        ],
        compiler_params=pltpu.CompilerParams(vmem_limit_bytes=48 * 1024 * 1024),
        cost_estimate=pl.CostEstimate(flops=1, bytes_accessed=1, transcendentals=0),
    )(lengths, lam, rot, grad_headed.reshape(dims + (2 * DH,)), cos_table, sin_table, gain)


TILE = 256


def tile_rows(rows):
    return next(t for t in (TILE, 128, 64, 32, 16) if rows % t == 0)


def row_call(
    kernel, cores, rows_in, whole_in, half_in, rows_out, half_out, shared=(), sums=()
):
    total = rows_in[0].shape[0]
    count = total if cores is None else total // 2
    tile = tile_rows(count)
    steps = count // tile
    first = jnp.zeros((1,), jnp.int32) if cores is None else cores * steps
    params = dict(memory_space=pltpu.VMEM)

    def of_all(cols):
        return pl.BlockSpec((tile, cols), lambda i, first: (first[0] + i, 0), **params)

    def of_half(cols):
        return pl.BlockSpec((tile, cols), lambda i, first: (i, 0), **params)

    n_in = len(rows_in) + len(whole_in) + len(half_in)

    def body_kernel(first, *refs):
        kernel(*refs[:n_in], *refs[n_in + len(shared) :])

    return pl.pallas_call(
        body_kernel,
        grid_spec=pltpu.PrefetchScalarGridSpec(
            num_scalar_prefetch=1,
            grid=(steps,),
            in_specs=[of_all(v.shape[1]) for v in rows_in]
            + [pl.BlockSpec(v.shape, lambda i, first: (0, 0), **params) for v in whole_in]
            + [of_half(v.shape[1]) for v in half_in]
            + [pl.BlockSpec(memory_space=pl.ANY) for _ in shared],
            out_specs=[of_all(c) for c, _ in rows_out]
            + [of_half(c) for c, _ in half_out]
            + [pl.BlockSpec(shape, lambda i, first: (0, 0), **params) for shape, _ in sums],
        ),
        out_shape=[jax.ShapeDtypeStruct((total, c), d) for c, d in rows_out]
        + [jax.ShapeDtypeStruct((count, c), d) for c, d in half_out]
        + [jax.ShapeDtypeStruct(shape, d) for shape, d in sums],
        input_output_aliases={1 + n_in + i: i for i in range(len(shared))},
        compiler_params=pltpu.CompilerParams(vmem_limit_bytes=56 * 1024 * 1024),
        cost_estimate=pl.CostEstimate(flops=1, bytes_accessed=1, transcendentals=0),
    )(first, *rows_in, *whole_in, *half_in, *shared)


def norm_product_kernel(x_ref, gain_ref, weight_ref, inverse_ref, normed_ref, out_ref):
    values = x_ref[...].astype(f32)
    inverse = inverse_rms(values)
    normed = (values * inverse * gain_ref[...]).astype(bf16)
    inverse_ref[...] = inverse
    normed_ref[...] = normed
    out_ref[...] = product(normed, weight_ref[...])


def column_pieces(refs, units):
    column = 0
    found, late = [], None
    for ref in refs:
        cols = ref.shape[1]
        if ref.shape[0] == units:
            if late is None:
                late = ref
                continue
            found.append((column, late[...], ref[...]))
            late = None
        else:
            found.append((column, ref[:units], ref[units:]))
        column += cols
    return found


def gate_up_kernel(x_ref, *refs):
    *pieces, gate_ref, up_ref, hidden_ref = refs
    gate = up = 0.0
    for start, gate_part, up_part in column_pieces(pieces, gate_ref.shape[1]):
        values = x_ref[:, start : start + gate_part.shape[1]]
        gate += against(values, gate_part)
        up += against(values, up_part)
    gate_ref[...] = gate
    up_ref[...] = up
    hidden_ref[...] = (gate * jax.nn.sigmoid(gate) * up).astype(bf16)


def add_other(value, other):
    return value + other[0][...].astype(f32) if other else value


def product_kernel(x_ref, weight_ref, *refs):
    refs[-1][...] = add_other(product(x_ref[...], weight_ref[...]), refs[:-1]).astype(bf16)


def gate_up_back_kernel(n_pieces, grad_ref, gate_ref, up_ref, down_ref, *refs):
    pieces, other, (gate_out, up_out, out_ref) = refs[:n_pieces], refs[n_pieces:-3], refs[-3:]
    grad_hidden = against(grad_ref[...], down_ref[...])
    gate = gate_ref[...]
    share = jax.nn.sigmoid(gate)
    grad_gate = grad_hidden * up_ref[...] * share * (1.0 + gate * (1.0 - share))
    grad_gate = grad_gate.astype(bf16)
    grad_up = (grad_hidden * (gate * share)).astype(bf16)
    gate_out[...] = grad_gate
    up_out[...] = grad_up
    for start, gate_part, up_part in column_pieces(pieces, gate_ref.shape[1]):
        cols = slice(start, start + gate_part.shape[1])
        grad = product(grad_gate, gate_part) + product(grad_up, up_part)
        if other:
            grad += other[0][:, cols].astype(f32)
        out_ref[:, cols] = grad.astype(bf16)


def place_units_kernel(depth, team, grad_ref, gate_ref, up_ref):
    shard = gate_ref.shape[0]
    units = grad_ref.shape[1] // 2
    part = units // depth
    for source in range(team):
        rows = grad_ref[source * shard : (source + 1) * shard, :].astype(f32)
        for first, out_ref in ((0, gate_ref), (units, up_ref)):
            for z in range(depth):
                column = (z * team + source) * part
                start = first + z * part
                out_ref[:, column : column + part] = rows[:, start : start + part]


def place_units(grad, depth, team):
    shape = (grad.shape[0] // team, team * grad.shape[1] // 2)
    return pl.pallas_call(
        functools.partial(place_units_kernel, depth, team),
        out_shape=[jax.ShapeDtypeStruct(shape, f32)] * 2,
        compiler_params=pltpu.CompilerParams(vmem_limit_bytes=40 * 1024 * 1024),
        cost_estimate=pl.CostEstimate(flops=1, bytes_accessed=1, transcendentals=0),
    )(grad)


def against_kernel(grad_ref, weight_ref, out_ref):
    out_ref[...] = against(grad_ref[...], weight_ref[...]).astype(bf16)


def inputs_back_kernel(grad_ref, x_ref, inverse_ref, weight_ref, other_ref, out_ref, sum_ref):
    @pl.when(pl.program_id(0) == 0)
    def _():
        sum_ref[...] = jnp.zeros_like(sum_ref)

    grad = against(grad_ref[...], weight_ref[...]) + other_ref[...].astype(f32)
    out_ref[...] = grad.astype(bf16)
    part = grad * (x_ref[...].astype(f32) * inverse_ref[...])
    sum_ref[...] += part.reshape(-1, 8, part.shape[1]).sum(axis=0)


def columns_kernel(left_ref, right_ref, *refs):
    *other, out_ref, total = refs
    step = pl.program_id(0)

    @pl.when(step == 0)
    def _():
        total[...] = contract_rows(left_ref[...], right_ref[...])

    @pl.when(step > 0)
    def _():
        total[...] += contract_rows(left_ref[...], right_ref[...])

    @pl.when(step == pl.num_programs(0) - 1)
    def _():
        out_ref[...] = add_other(total[...], other).astype(bf16)


def columns_call(left, right, *other):
    rows = left.shape[0]
    tile = next(t for t in (1024, 512, 384, 256, 192, 128, 64, 32, 16) if rows % t == 0)
    shape = (left.shape[1], right.shape[1])
    whole = pl.BlockSpec(shape, lambda k: (0, 0))
    return pl.pallas_call(
        columns_kernel,
        grid=(rows // tile,),
        in_specs=[pl.BlockSpec((tile, v.shape[1]), lambda k: (k, 0)) for v in (left, right)]
        + [whole] * len(other),
        out_specs=whole,
        out_shape=jax.ShapeDtypeStruct(shape, bf16),
        scratch_shapes=[pltpu.VMEM(shape, f32)],
        compiler_params=pltpu.CompilerParams(vmem_limit_bytes=56 * 1024 * 1024),
        cost_estimate=pl.CostEstimate(flops=1, bytes_accessed=1, transcendentals=0),
    )(left, right, *other)


def shift(depth, step):
    return [(i, (i + step) % depth) for i in range(depth)]


def after(value, *others):
    return lax.optimization_barrier((value, *others))[0]


def permute(value, depth, step):
    return lax.ppermute(value, "z", shift(depth, step))


class Gather:
    def __init__(self, block, depth, hold=None):
        self.block, self.depth = block, depth
        self.near = [(block, block)]
        for _ in range((depth - 1) // 2):
            above, below = self.near[-1]
            pair = (permute(above, depth, -1), permute(below, depth, 1))
            self.near.append(pair if hold is None else hold(pair))
        self.far = None
        if depth % 2 == 0:
            above, below = self.near[-1]
            half = block.shape[0] // 2
            self.far = (permute(above[:half], depth, -1), permute(below[half:], depth, 1))

    def pieces(self):
        above = [pair[0] for pair in self.near[1:]]
        below = [pair[1] for pair in self.near[:0:-1]]
        return [self.block] + above + list(self.far or ()) + below

    def joined(self, axis, *others):
        near, far = self.near[1:], self.far
        if others:
            near, far, _ = lax.optimization_barrier((near, far, others))
        middle = [] if far is None else [jnp.concatenate(far, axis=0)]
        above = [pair[0] for pair in near]
        below = [pair[1] for pair in near[::-1]]
        return jnp.concatenate([self.block] + above + middle + below, axis=axis)

    def first(self):
        return self.near[-1]

    def last(self):
        return self.near[-1] if self.far is None else self.far


class Scatter:
    def __init__(self, tops, bottoms):
        depth = len(tops)
        self.pairs = [
            [(tops[k], bottoms[-k % depth]) for k in range(depth // 2 + 1)],
            [(bottoms[k], tops[-k % depth]) for k in range((depth - 1) // 2 + 1)],
        ]
        self.depth = depth
        self.first = self.move(self.pairs[0][-1]) if depth > 1 else None

    def move(self, pair):
        return (permute(pair[0], self.depth, 1), permute(pair[1], self.depth, -1))

    def chain(self, pairs, moved):
        for pair in pairs[-2:0:-1]:
            moved = self.move(
                tuple((a.astype(f32) + b.astype(f32)).astype(bf16) for a, b in zip(pair, moved))
            )
        return moved

    def plain(self):
        pairs = self.pairs[1]
        self.second = self.chain(pairs, self.move(pairs[-1])) if len(pairs) > 1 else None
        return self.second

    def added(self, *others):
        pairs = self.pairs[0]
        self.third = self.chain(pairs, after(self.first, *others)) if self.depth > 1 else None
        return self.third

    def total(self, *others):
        top, bottom = self.pairs[0][0]
        top, bottom = top.astype(f32), bottom.astype(f32)
        third, second, _ = lax.optimization_barrier((self.third, self.second, others))
        for pair, swap in ((third, False), (second, True)):
            if pair is not None:
                up, down = pair[::-1] if swap else pair
                top, bottom = top + up.astype(f32), bottom + down.astype(f32)
        return top, bottom


def scatter_straight(blocks):
    depth = len(blocks)
    moved = [permute(blocks[k], depth, k) for k in range(1, depth)]
    return sum((v.astype(f32) for v in moved), blocks[0].astype(f32))


def halves(blocks):
    half = blocks[0].shape[0] // 2
    return [block[:half] for block in blocks], [block[half:] for block in blocks]


def turn_blocks(values, depth, axis, forth=True):
    size = values.shape[axis]
    here = lax.axis_index("z")
    start = (here if forth else (depth - here) % depth) * (size // depth)
    return lax.dynamic_slice_in_dim(
        jnp.concatenate([values, values], axis=axis), start, size, axis
    )


def gather_rows(block):
    return lax.all_gather(block, ROWS, axis=0, tiled=True)


def exchange(values, split, joined, order=ROWS):
    return lax.all_to_all(values, order, split_axis=split, concat_axis=joined, tiled=True)


def split_cores(values, axis=0):
    count = values.shape[axis] // 2
    mine = lax.axis_index("c")
    return [
        lax.dynamic_slice_in_dim(values, core * count, count, axis) for core in (1 - mine, mine)
    ]


def across(values):
    return lax.ppermute(values, "c", [(0, 1), (1, 0)])


def over_chips(total):
    return lax.psum_scatter(total, ("y", "x"), scatter_dimension=0, tiled=True)


def body(
    inputs, cotangent, lengths, w_query, w_key, w_value, w_out, w_gate, w_up, w_down,
    norm_attn, norm_head, norm_ffn, lambda_params, *, depth,
):
    batches, _, rows, width = inputs.shape
    team = H
    chips = team // 2
    shard = w_query.shape[0]
    hidden_shard = w_down.shape[0]
    own_rows = batches * rows
    dims = (2, chips, batches, rows)
    total_rows = 2 * rows
    places = depth * team
    units = depth * hidden_shard
    turned = functools.partial(turn_blocks, depth=depth)

    def natural(blocks):
        shape = blocks.shape
        blocks = blocks.reshape((2, chips, shape[0] // team) + shape[1:])
        return jnp.swapaxes(blocks, 0, 1).reshape(shape)

    def by_core(blocks):
        shape = blocks.shape
        blocks = blocks.reshape((chips, 2, shape[0] // team) + shape[1:])
        return jnp.swapaxes(blocks, 0, 1).reshape(shape)

    x_own = inputs.reshape(own_rows, width)
    x_all = gather_rows(turned(x_own, axis=1))

    qkv = jnp.concatenate(
        [w.reshape(shard, H, 2 * DH) for w in (w_query, w_key, w_value)], axis=2
    )
    qkv = exchange(qkv.transpose(1, 0, 2).reshape(H * shard, 6 * DH), 0, 0)

    small = jnp.concatenate(
        [
            norm_attn.astype(f32), norm_head.astype(f32), norm_ffn.astype(f32),
            lambda_params.astype(f32), lengths[:, 0].astype(f32),
        ]
    )[None]
    small = lax.all_gather(after(small, natural(qkv)), TEAM, axis=0, tiled=True)
    length_all = small[:, -batches:].reshape(chips, 2, batches)[:, 0].astype(jnp.int32)
    far_small = [permute(small, depth, -k) for k in range(1, depth)]
    out_ring = Gather(w_out, depth, lambda near: after(near, natural(qkv)))
    qkv_ring = Gather(
        natural(qkv),
        depth,
        lambda near: after(near, far_small, out_ring.last()),
    )
    small = jnp.concatenate([small] + far_small, axis=0).reshape(depth, team, -1)
    small = turned(small, axis=0, forth=False)
    qkv_near = qkv_ring.first()
    out_w = out_ring.joined(0).reshape(depth, shard, width)
    out_w = lax.all_gather(out_w, TEAM, axis=1, tiled=False)
    out_w = turned(out_w, axis=0, forth=False).reshape(width, width)

    def by_units(w):
        w = w.reshape(shard, depth, team, hidden_shard).transpose(2, 0, 1, 3)
        return w.reshape(team * shard, units)

    gate_up = jnp.concatenate([by_units(w_gate), by_units(w_up)], axis=1)
    n_lam = lambda_params.shape[0]
    gain_attn = small[:, :, :shard].reshape(1, width)
    gain_head = small[:, :, shard : 2 * shard].reshape(H, 2 * DH)
    gain_ffn = small[:, :, 2 * shard : 3 * shard].reshape(1, width)
    lam_parts = small[:, :, 3 * shard : 3 * shard + n_lam].reshape(4, DH)
    first_exp = jnp.exp(jnp.sum(lam_parts[0] * lam_parts[1]))
    second_exp = jnp.exp(jnp.sum(lam_parts[2] * lam_parts[3]))
    lam = (first_exp - second_exp + lambda_init)[None]
    head = lax.axis_index(ROWS)
    gain_mine = lax.dynamic_index_in_dim(gain_head, head, 0) * (1.0 - lambda_init)

    frequency = rope_base ** (-jnp.arange(DH // 2, dtype=f32) / (DH // 2))
    angles = jnp.arange(total_rows, dtype=f32)[:, None] * frequency[None, :]
    cos_table = jnp.concatenate([jnp.cos(angles)] * 2, axis=1)
    sine = jnp.sin(angles)
    sin_table = jnp.concatenate([-sine, sine], axis=1)

    gate_up = exchange(after(gate_up, *qkv_near), 0, 0, TEAM).T
    x_all = after(x_all, *qkv_ring.last(), gate_up)
    inverse_all, normed_one, raw = row_call(
        norm_product_kernel, None, [x_all], [turned(gain_attn, axis=1), qkv_ring.joined(0)], [],
        [(1, f32), (width, bf16), (6 * DH, f32)], [],
    )
    gate_up_ring = Gather(gate_up, depth)
    rot, headed = attend(length_all, lam, raw, cos_table, sin_table, gain_mine, dims)
    headed_own = exchange(headed.reshape(team * own_rows, 2 * DH), 0, 1)
    headed_own = after(headed_own, *gate_up_ring.first())

    x_own = x_own.astype(f32)
    residual = x_own + product(headed_own, out_w)
    inverse_two = inverse_rms(residual)
    unit_two = residual * inverse_two
    normed_two = gather_rows(turned((unit_two * gain_ffn).astype(bf16), axis=1))

    positions = lax.axis_index("c") * rows + jnp.arange(rows, dtype=jnp.int32)
    valid = (positions[None, :] < lengths).reshape(own_rows, 1)
    grad_own = jnp.where(valid, cotangent.reshape(own_rows, width), 0)
    grad_all = gather_rows(grad_own)

    mine = lax.axis_index("c")[None].astype(jnp.int32)
    gate_up_w = gate_up_ring.pieces()
    gate_val, up_val, hidden = row_call(
        gate_up_kernel, None, [normed_two], gate_up_w, [],
        [(units, f32), (units, f32), (units, bf16)], [],
    )
    down_ring = Gather(
        after(w_down, *gate_up_ring.last()), depth, lambda near: after(near, hidden)
    )
    down_w = turned(down_ring.joined(0), axis=0, forth=False)

    (sent,) = row_call(product_kernel, 1 - mine, [hidden], [down_w], [], [], [(width, bf16)])
    (out_rows,) = row_call(
        product_kernel, mine, [hidden], [down_w], [across(sent)], [], [(width, bf16)]
    )
    grad_all = after(grad_all, out_rows)
    out_rows = over_chips(out_rows)

    grads = [(units, bf16), (units, bf16)]
    back_kernel = functools.partial(gate_up_back_kernel, len(gate_up_w))
    back_in = [grad_all, gate_val, up_val]
    *grad_gate_up, sent = row_call(
        back_kernel, 1 - mine, back_in, [down_w, *gate_up_w], [], grads, [(width, bf16)]
    )
    grad_w_down = columns_call(hidden, after(grad_all, sent))
    *grad_gate_up, grad_two = row_call(
        back_kernel, mine, back_in, [down_w, *gate_up_w],
        [after(across(sent), grad_w_down)], grads, [(width, bf16)], grad_gate_up,
    )
    down_blocks = grad_w_down.reshape(depth, hidden_shard, width)
    down_back = Scatter(
        *halves(
            [
                lax.dynamic_index_in_dim(down_blocks, (lax.axis_index("z") + k) % depth, 0, False)
                for k in range(depth)
            ]
        )
    )
    grad_two = after(grad_two, *down_back.first)
    down_back.plain()
    grad_w_gate, grad_w_up = (
        columns_call(after(v, grad_two), normed_two) for v in grad_gate_up
    )
    down_back.added(*down_back.second, grad_w_gate)
    gate_up_back = Scatter(
        *(jnp.split(v, depth, axis=1) for v in (grad_w_gate, grad_w_up))
    )
    gate_up_back.plain()
    gate_up_back.added()
    grad_two = after(
        over_chips(after(grad_two, out_rows)), grad_w_gate, grad_w_up, *gate_up_back.first,
        *down_back.second, *down_back.third,
    )
    grad_two = turned(grad_two, axis=1, forth=False).astype(f32)
    grad_w_down = jnp.concatenate(down_back.total(), axis=0)

    grad_norm_ffn = jnp.sum(grad_two * unit_two, axis=0)
    grad_resid = grad_own.astype(f32) + norm_back(grad_two * gain_ffn, unit_two, inverse_two)
    grad_branch = grad_resid.astype(bf16)
    sent_heads = against(grad_branch, out_w).astype(bf16)
    grad_headed = exchange(sent_heads, 1, 0)
    headed_cores = headed_own.reshape(own_rows, depth, chips, 2, shard).transpose(0, 3, 2, 1, 4)
    headed_cores = turned(headed_cores, axis=3).reshape(own_rows, width)
    theirs, own = split_cores(headed_cores, 1)
    branch = after(grad_branch, sent_heads)
    sent = across(columns_call(theirs, branch))
    grad_w_out = columns_call(own, branch, after(sent, grad_headed))
    grad_headed = after(grad_headed, grad_w_out)
    grad_w_out = over_chips(after(grad_w_out, *gate_up_back.second))
    grad_raw, grad_head, grad_lam = attend_back(
        length_all, lam, rot, grad_headed, cos_table, -sin_table, gain_mine, dims
    )
    grad_raw = grad_raw.reshape(team * own_rows, 6 * DH)
    out_rows = after(out_rows, grad_raw)
    output = jnp.where(valid, residual + out_rows.astype(f32), 0.0).astype(bf16)
    qkv_w = qkv_ring.joined(0)
    (sent,) = row_call(against_kernel, 1 - mine, [grad_raw], [qkv_w], [], [], [(width, bf16)])
    sent = after(sent, *gate_up_back.third)
    grad_w_gate_up = jnp.concatenate([v.astype(bf16).T for v in gate_up_back.total()], axis=1)
    grad_w_gate_up = exchange(grad_w_gate_up, 0, 0, TEAM)
    grad_qkv = columns_call(normed_one, after(grad_raw, sent))
    qkv_back = Scatter(*halves(jnp.split(grad_qkv, depth, axis=0)))
    grad_one, norm_sums = row_call(
        inputs_back_kernel, mine, [grad_raw, x_all, inverse_all], [qkv_w],
        [after(across(sent), grad_qkv)], [], [(width, bf16)], sums=[((8, width), f32)],
    )
    grad_norm_attn = turned(jnp.sum(norm_sums, axis=0), axis=0, forth=False)
    grad_one = over_chips(after(grad_one, grad_w_gate_up, *qkv_back.first))
    grad_w_gate, grad_w_up = place_units(grad_w_gate_up, depth, team)
    qkv_back.plain()
    qkv_back.added(grad_w_gate_up)
    grad_w_out = scatter_straight(jnp.split(grad_w_out, depth, axis=0))
    grad_lam = grad_lam[0, 0]
    grad_lambda = jnp.concatenate(
        [
            grad_lam * first_exp * lam_parts[1],
            grad_lam * first_exp * lam_parts[0],
            -grad_lam * second_exp * lam_parts[3],
            -grad_lam * second_exp * lam_parts[2],
        ]
    )
    grad_head = grad_head * (1.0 - lambda_init)
    head_full = lax.dynamic_update_slice(jnp.zeros((H, 2 * DH), f32), grad_head, (head, 0))
    small_grads = jnp.concatenate(
        [
            grad_norm_attn.reshape(places, shard),
            head_full.reshape(places, shard),
            grad_norm_ffn.reshape(places, shard),
            grad_lambda.reshape(places, n_lam),
        ],
        axis=1,
    )
    small_grads = small_grads.reshape(depth, team, -1).swapaxes(0, 1).reshape(places, -1)
    small_grads = exchange(small_grads, 0, 0, TEAM).reshape(team, depth, -1).sum(axis=0)
    small_grads = lax.all_to_all(small_grads, "z", 0, 0, tiled=True).sum(axis=0)

    grad_qkv = exchange(by_core(jnp.concatenate(qkv_back.total(small_grads, grad_w_gate, grad_w_up, grad_w_out), axis=0)).astype(bf16), 0, 0).astype(f32)
    grad_qkv = grad_qkv.reshape(H, shard, 3, 2 * DH).transpose(2, 1, 0, 3)
    grad_qkv = grad_qkv.reshape(3, shard, width)

    inverse_one = inverse_rms(x_own)
    grad_one = after(grad_one, small_grads, grad_w_gate, grad_w_up, grad_w_out)
    grad_one = turned(grad_one, axis=1, forth=False).astype(f32)
    unit_one = x_own * inverse_one
    input_grad = (
        grad_resid + norm_back(grad_one * gain_attn, unit_one, inverse_one)
    ).astype(bf16)

    return (
        output.reshape(inputs.shape),
        input_grad.reshape(inputs.shape),
        grad_qkv[0],
        grad_qkv[1],
        grad_qkv[2],
        grad_w_out,
        grad_w_gate,
        grad_w_up,
        grad_w_down,
        small_grads[:shard],
        small_grads[shard : 2 * shard],
        small_grads[2 * shard : 3 * shard],
        small_grads[3 * shard :],
    )


def solution(mesh):
    cores = mesh.shape["in"]
    depth = mesh.shape["grp"] * cores // H
    split = Mesh(mesh.devices.reshape(depth, 2, H // (2 * cores), cores), EVERY)
    group = ("z", "y", "x")
    data = P(None, group, "c", None)
    matrix = P(EVERY, None)
    vector = P(EVERY)
    return jax.shard_map(
        functools.partial(body, depth=depth),
        mesh=split,
        in_specs=(data, data, P(None, group)) + (matrix,) * 7 + (vector,) * 4,
        out_specs=(data, data) + (matrix,) * 7 + (vector,) * 4,
        check_vma=False,
    )
```

```python
import functools
import math

import jax
import jax.numpy as jnp
from jax import lax
from jax.experimental import pallas as pl
from jax.experimental.pallas import tpu as pltpu
from jax.sharding import Mesh
from jax.sharding import PartitionSpec as P

H = 8
DH = 128
TEAM = ("y", "x", "c")
ROWS = ("c", "y", "x")
EVERY = ("z", "y", "x", "c")

epsilon = 1e-05
lambda_init = 0.8 - 0.6 * math.exp(-3.3)
rope_base = 10000.0
score_scale = 1.0 / math.sqrt(DH)
bf16 = jnp.bfloat16
f32 = jnp.float32


def product(left, right):
    return jnp.dot(left, right, preferred_element_type=f32)


def contract_rows(left, right):
    return lax.dot_general(left, right, (((0,), (0,)), ((), ())), preferred_element_type=f32)


def against(left, right):
    return lax.dot_general(left, right, (((1,), (1,)), ((), ())), preferred_element_type=f32)


def inverse_rms(values):
    return lax.rsqrt(jnp.mean(values * values, axis=-1, keepdims=True) + epsilon)


def norm_back(grad_unit, unit_vals, inverse):
    return inverse * (
        grad_unit - unit_vals * jnp.mean(grad_unit * unit_vals, axis=-1, keepdims=True)
    )


def turn(values, cos_table, sin_table):
    return values * cos_table + pltpu.roll(values, DH // 2, 1) * sin_table


def softmax_block(query, key, allowed):
    scores = jnp.where(allowed, against(query, key) * score_scale, -1e30)
    terms = jnp.exp(scores - jnp.max(scores, axis=-1, keepdims=True))
    return terms / jnp.sum(terms, axis=-1, keepdims=True)


def allowed_block(start, rows, keys, length):
    row = start + lax.broadcasted_iota(jnp.int32, (rows, keys), 0)
    col = lax.broadcasted_iota(jnp.int32, (rows, keys), 1)
    return (col <= row) & (col < length)


def attend_kernel(len_ref, lam_ref, raw_ref, cos_ref, sin_ref, gain_ref, rot_ref, headed_ref, probs_ref, kept_ref):
    for batch in range(raw_ref.shape[2]):
        length = len_ref[pl.program_id(0), batch]
        lam = lam_ref[0]
        halves, rows = raw_ref.shape[0], raw_ref.shape[3]
        total = halves * rows
        raw = raw_ref[:, 0, batch].reshape(total, 6 * DH)
        cos_table, sin_table = cos_ref[...], sin_ref[...]
        turned = [
            turn(raw[:, part * DH : (part + 1) * DH], cos_table, sin_table).astype(bf16)
            for part in range(4)
        ]
        value = raw[:, 4 * DH :].astype(bf16)
        rot_ref[:, 0, batch] = jnp.concatenate(turned + [value], axis=1).reshape(halves, rows, 6 * DH)
        gain = gain_ref[...]
        step = 128
        parts = []
        for start in range(0, total, step):
            keys = start + step
            mask = allowed_block(start, step, keys, length)
            first = softmax_block(turned[0][start:keys], turned[2][:keys], mask)
            second = softmax_block(turned[1][start:keys], turned[3][:keys], mask)
            combined = (first - lam * second).astype(bf16)
            attended = product(combined, value[:keys])
            probs_ref[0, batch, 0, start:keys, :keys] = first
            probs_ref[0, batch, 1, start:keys, :keys] = second
            kept_ref[0, batch, start:keys] = attended
            parts.append((attended * inverse_rms(attended) * gain).astype(bf16))
        headed_ref[:, 0, batch] = jnp.concatenate(parts, axis=0).reshape(halves, rows, 2 * DH)


def attend_back_kernel(
    lam_ref, rot_ref, probs_ref, kept_ref, grad_ref, cos_ref, sin_ref, gain_ref,
    out_ref, head_ref, lam_out_ref, all_keys, all_values,
):
    @pl.when(pl.program_id(0) == 0)
    def _():
        head_ref[...] = jnp.zeros_like(head_ref)
        lam_out_ref[...] = jnp.zeros_like(lam_out_ref)

    for batch in range(rot_ref.shape[2]):
        grad_key, grad_value = all_keys.at[batch], all_values.at[batch]
        lam = lam_ref[0]
        halves, rows = rot_ref.shape[0], rot_ref.shape[3]
        total = halves * rows
        rot = rot_ref[:, 0, batch].reshape(total, 6 * DH)
        grad_headed = grad_ref[:, 0, batch].reshape(total, 2 * DH).astype(f32)
        cos_table, sin_table = cos_ref[...], sin_ref[...]
        query = [rot[:, :DH], rot[:, DH : 2 * DH]]
        key = [rot[:, 2 * DH : 3 * DH], rot[:, 3 * DH : 4 * DH]]
        value = rot[:, 4 * DH :]
        gain = gain_ref[...]
        step = 128
        grad_query = [[], []]
        for start in reversed(range(0, total, step)):
            keys = start + step
            first = probs_ref[0, batch, 0, start:keys, :keys]
            second = probs_ref[0, batch, 1, start:keys, :keys]
            combined = (first - lam * second).astype(bf16)
            attended = kept_ref[0, batch, start:keys]
            inverse = inverse_rms(attended)
            unit = attended * inverse
            grad_head = grad_headed[start:keys]
            head_ref[...] += jnp.sum(grad_head * unit, axis=0, keepdims=True)
            grad_attended = norm_back(grad_head * gain, unit, inverse).astype(bf16)
            grad_comb = against(grad_attended, value[:keys])
            value_part = contract_rows(combined, grad_attended)
            inner = [
                jnp.sum(grad_comb * first, axis=-1, keepdims=True),
                jnp.sum(grad_comb * second, axis=-1, keepdims=True),
            ]
            lam_out_ref[...] -= jnp.sum(inner[1], axis=0, keepdims=True)
            grad_scores = [
                (first * (grad_comb - inner[0])).astype(bf16),
                (-lam * second * (grad_comb - inner[1])).astype(bf16),
            ]
            if keys == total:
                grad_value[...] = value_part
            else:
                grad_value[:keys] += value_part
            for k in range(2):
                key_part = contract_rows(grad_scores[k], query[k][start:keys])
                cols = slice(k * DH, (k + 1) * DH)
                if keys == total:
                    grad_key[:, cols] = key_part
                else:
                    grad_key[:keys, cols] += key_part
                grad_query[k].append(product(grad_scores[k], key[k][:keys]) * score_scale)
        turned = [
            turn(jnp.concatenate(grad_query[k][::-1], axis=0), cos_table, sin_table).astype(bf16)
            for k in range(2)
        ] + [
            turn(grad_key[:, k * DH : (k + 1) * DH] * score_scale, cos_table, sin_table).astype(bf16)
            for k in range(2)
        ]
        out_ref[:, 0, batch] = jnp.concatenate(
            turned + [grad_value[...].astype(bf16)], axis=1
        ).reshape(halves, rows, 6 * DH)


def row_spec(halves, batches, rows, cols):
    return pl.BlockSpec((halves, 1, batches, rows, cols), lambda j: (0, j, 0, 0, 0))


def whole_spec(shape):
    return pl.BlockSpec(shape, lambda j: (0,) * len(shape))


def slot_spec(*shape):
    return pl.BlockSpec((1,) + shape, lambda j: (j,) + (0,) * len(shape))


def attend(lengths, lam, raw, cos_table, sin_table, gain, dims):
    halves, slots, batches, rows = dims
    smem = pl.BlockSpec(memory_space=pltpu.SMEM)
    total = halves * rows
    return pl.pallas_call(
        attend_kernel,
        grid=(slots,),
        in_specs=[
            smem, smem, row_spec(halves, batches, rows, 6 * DH),
            whole_spec(cos_table.shape), whole_spec(sin_table.shape), whole_spec(gain.shape),
        ],
        out_specs=[
            row_spec(halves, batches, rows, 6 * DH), row_spec(halves, batches, rows, 2 * DH),
            slot_spec(batches, 2, total, total), slot_spec(batches, total, 2 * DH),
        ],
        out_shape=[
            jax.ShapeDtypeStruct(dims + (6 * DH,), bf16),
            jax.ShapeDtypeStruct(dims + (2 * DH,), bf16),
            jax.ShapeDtypeStruct((slots, batches, 2, total, total), f32),
            jax.ShapeDtypeStruct((slots, batches, total, 2 * DH), f32),
        ],
        compiler_params=pltpu.CompilerParams(vmem_limit_bytes=48 * 1024 * 1024),
        cost_estimate=pl.CostEstimate(flops=1, bytes_accessed=1, transcendentals=0),
    )(lengths, lam, raw.reshape(dims + (6 * DH,)), cos_table, sin_table, gain)


def attend_back(lam, rot, probs, kept, grad_headed, cos_table, sin_table, gain, dims):
    halves, slots, batches, rows = dims
    smem = pl.BlockSpec(memory_space=pltpu.SMEM)
    return pl.pallas_call(
        attend_back_kernel,
        grid=(slots,),
        in_specs=[
            smem, row_spec(halves, batches, rows, 6 * DH), slot_spec(*probs.shape[1:]),
            slot_spec(*kept.shape[1:]), row_spec(halves, batches, rows, 2 * DH),
            whole_spec(cos_table.shape), whole_spec(sin_table.shape), whole_spec(gain.shape),
        ],
        out_specs=[
            row_spec(halves, batches, rows, 6 * DH), whole_spec((1, 2 * DH)), whole_spec((1, 128)),
        ],
        out_shape=[
            jax.ShapeDtypeStruct(dims + (6 * DH,), bf16),
            jax.ShapeDtypeStruct((1, 2 * DH), f32),
            jax.ShapeDtypeStruct((1, 128), f32),
        ],
        scratch_shapes=[
            pltpu.VMEM((batches, halves * rows, 2 * DH), f32),
            pltpu.VMEM((batches, halves * rows, 2 * DH), f32),
        ],
        compiler_params=pltpu.CompilerParams(vmem_limit_bytes=48 * 1024 * 1024),
        cost_estimate=pl.CostEstimate(flops=1, bytes_accessed=1, transcendentals=0),
    )(lam, rot, probs, kept, grad_headed.reshape(dims + (2 * DH,)), cos_table, sin_table, gain)


TILE = 512


def tile_rows(rows):
    return next(t for t in (TILE, 256, 128, 64, 32, 16) if rows % t == 0)


def row_call(
    kernel, cores, rows_in, whole_in, half_in, rows_out, half_out, shared=(), sums=()
):
    total = rows_in[0].shape[0]
    count = total if cores is None else total // 2
    tile = tile_rows(count)
    steps = count // tile
    first = jnp.zeros((1,), jnp.int32) if cores is None else cores * steps
    params = dict(memory_space=pltpu.VMEM)

    def of_all(cols):
        return pl.BlockSpec((tile, cols), lambda i, first: (first[0] + i, 0), **params)

    def of_half(cols):
        return pl.BlockSpec((tile, cols), lambda i, first: (i, 0), **params)

    n_in = len(rows_in) + len(whole_in) + len(half_in)

    def body_kernel(first, *refs):
        kernel(*refs[:n_in], *refs[n_in + len(shared) :])

    return pl.pallas_call(
        body_kernel,
        grid_spec=pltpu.PrefetchScalarGridSpec(
            num_scalar_prefetch=1,
            grid=(steps,),
            in_specs=[of_all(v.shape[1]) for v in rows_in]
            + [pl.BlockSpec(v.shape, lambda i, first: (0, 0), **params) for v in whole_in]
            + [of_half(v.shape[1]) for v in half_in]
            + [pl.BlockSpec(memory_space=pl.ANY) for _ in shared],
            out_specs=[of_all(c) for c, _ in rows_out]
            + [of_half(c) for c, _ in half_out]
            + [pl.BlockSpec(shape, lambda i, first: (0, 0), **params) for shape, _ in sums],
        ),
        out_shape=[jax.ShapeDtypeStruct((total, c), d) for c, d in rows_out]
        + [jax.ShapeDtypeStruct((count, c), d) for c, d in half_out]
        + [jax.ShapeDtypeStruct(shape, d) for shape, d in sums],
        input_output_aliases={1 + n_in + i: i for i in range(len(shared))},
        compiler_params=pltpu.CompilerParams(vmem_limit_bytes=56 * 1024 * 1024),
        cost_estimate=pl.CostEstimate(flops=1, bytes_accessed=1, transcendentals=0),
    )(first, *rows_in, *whole_in, *half_in, *shared)


def norm_product_kernel(x_ref, gain_ref, weight_ref, inverse_ref, normed_ref, out_ref):
    values = x_ref[...].astype(f32)
    inverse = inverse_rms(values)
    normed = (values * inverse * gain_ref[...]).astype(bf16)
    inverse_ref[...] = inverse
    normed_ref[...] = normed
    out_ref[...] = product(normed, weight_ref[...])


def column_pieces(refs, units):
    column = 0
    found, late = [], None
    for ref in refs:
        cols = ref.shape[1]
        if ref.shape[0] == units:
            if late is None:
                late = ref
                continue
            found.append((column, late[...], ref[...]))
            late = None
        else:
            found.append((column, ref[:units], ref[units:]))
        column += cols
    return found


def gate_up_kernel(x_ref, *refs):
    *pieces, gate_ref, up_ref, hidden_ref = refs
    gate = up = 0.0
    for start, gate_part, up_part in column_pieces(pieces, gate_ref.shape[1]):
        values = x_ref[:, start : start + gate_part.shape[1]]
        gate += against(values, gate_part)
        up += against(values, up_part)
    gate_ref[...] = gate
    up_ref[...] = up
    hidden_ref[...] = (gate * jax.nn.sigmoid(gate) * up).astype(bf16)


def add_other(value, other):
    return value + other[0][...].astype(f32) if other else value


def product_kernel(x_ref, weight_ref, *refs):
    refs[-1][...] = add_other(product(x_ref[...], weight_ref[...]), refs[:-1]).astype(bf16)


def gate_up_back_kernel(n_pieces, grad_ref, gate_ref, up_ref, down_ref, *refs):
    pieces, other, (gate_out, up_out, out_ref) = refs[:n_pieces], refs[n_pieces:-3], refs[-3:]
    tile = grad_ref.shape[0]
    block = min(tile, 256)
    blocks = [slice(start, start + block) for start in range(0, tile, block)]
    hidden = [against(grad_ref[at, :], down_ref[...]) for at in blocks]
    grads = []
    for at, grad_hidden in zip(blocks, hidden, strict=True):
        gate = gate_ref[at, :]
        share = jax.nn.sigmoid(gate)
        grad_gate = grad_hidden * up_ref[at, :] * share * (1.0 + gate * (1.0 - share))
        grad_gate = grad_gate.astype(bf16)
        grad_up = (grad_hidden * (gate * share)).astype(bf16)
        gate_out[at, :] = grad_gate
        up_out[at, :] = grad_up
        grads.append((grad_gate, grad_up))
    for at, (grad_gate, grad_up) in zip(blocks, grads, strict=True):
        for start, gate_part, up_part in column_pieces(pieces, gate_ref.shape[1]):
            cols = slice(start, start + gate_part.shape[1])
            grad = product(grad_gate, gate_part) + product(grad_up, up_part)
            if other:
                grad += other[0][at, cols].astype(f32)
            out_ref[at, cols] = grad.astype(bf16)


def place_units_kernel(depth, team, grad_ref, gate_ref, up_ref):
    shard = gate_ref.shape[0]
    units = grad_ref.shape[1] // 2
    part = units // depth
    for source in range(team):
        rows = grad_ref[source * shard : (source + 1) * shard, :].astype(f32)
        for first, out_ref in ((0, gate_ref), (units, up_ref)):
            for z in range(depth):
                column = (z * team + source) * part
                start = first + z * part
                out_ref[:, column : column + part] = rows[:, start : start + part]


def place_heads_kernel(grad_ref, *out_refs):
    shard = out_refs[0].shape[0]
    for head in range(H):
        rows = grad_ref[head * shard : (head + 1) * shard, :].astype(f32)
        for k, out_ref in enumerate(out_refs):
            out_ref[:, head * 2 * DH : (head + 1) * 2 * DH] = rows[:, k * 2 * DH : (k + 1) * 2 * DH]


def place_heads(grad, work):
    return pl.pallas_call(
        place_heads_kernel,
        out_shape=[jax.ShapeDtypeStruct((grad.shape[0] // H, H * 2 * DH), f32)] * 3,
        compiler_params=pltpu.CompilerParams(vmem_limit_bytes=40 * 1024 * 1024),
        cost_estimate=pl.CostEstimate(flops=work, bytes_accessed=work // 300, transcendentals=0),
    )(grad)


def place_units(grad, depth, team):
    shape = (grad.shape[0] // team, team * grad.shape[1] // 2)
    return pl.pallas_call(
        functools.partial(place_units_kernel, depth, team),
        out_shape=[jax.ShapeDtypeStruct(shape, f32)] * 2,
        compiler_params=pltpu.CompilerParams(vmem_limit_bytes=40 * 1024 * 1024),
        cost_estimate=pl.CostEstimate(flops=1, bytes_accessed=1, transcendentals=0),
    )(grad)


def against_kernel(grad_ref, weight_ref, out_ref):
    out_ref[...] = against(grad_ref[...], weight_ref[...]).astype(bf16)


def inputs_back_kernel(grad_ref, x_ref, inverse_ref, weight_ref, other_ref, out_ref, sum_ref):
    @pl.when(pl.program_id(0) == 0)
    def _():
        sum_ref[...] = jnp.zeros_like(sum_ref)

    grad = against(grad_ref[...], weight_ref[...]) + other_ref[...].astype(f32)
    out_ref[...] = grad.astype(bf16)
    part = grad * (x_ref[...].astype(f32) * inverse_ref[...])
    sum_ref[...] += part.reshape(-1, 8, part.shape[1]).sum(axis=0)


def columns_kernel(left_ref, right_ref, *refs):
    *other, out_ref, total = refs
    step = pl.program_id(0)

    @pl.when(step == 0)
    def _():
        total[...] = contract_rows(left_ref[...], right_ref[...])

    @pl.when(step > 0)
    def _():
        total[...] += contract_rows(left_ref[...], right_ref[...])

    @pl.when(step == pl.num_programs(0) - 1)
    def _():
        out_ref[...] = add_other(total[...], other).astype(bf16)


def columns_call(left, right, *other):
    rows = left.shape[0]
    tile = next(t for t in (1024, 512, 384, 256, 192, 128, 64, 32, 16) if rows % t == 0)
    shape = (left.shape[1], right.shape[1])
    whole = pl.BlockSpec(shape, lambda k: (0, 0))
    return pl.pallas_call(
        columns_kernel,
        grid=(rows // tile,),
        in_specs=[pl.BlockSpec((tile, v.shape[1]), lambda k: (k, 0)) for v in (left, right)]
        + [whole] * len(other),
        out_specs=whole,
        out_shape=jax.ShapeDtypeStruct(shape, bf16),
        scratch_shapes=[pltpu.VMEM(shape, f32)],
        compiler_params=pltpu.CompilerParams(vmem_limit_bytes=56 * 1024 * 1024),
        cost_estimate=pl.CostEstimate(flops=1, bytes_accessed=1, transcendentals=0),
    )(left, right, *other)


def shift(depth, step):
    return [(i, (i + step) % depth) for i in range(depth)]


def after(value, *others):
    return lax.optimization_barrier((value, *others))[0]


def permute(value, depth, step):
    return lax.ppermute(value, "z", shift(depth, step))


class Gather:
    def __init__(self, block, depth, hold=None):
        self.block, self.depth = block, depth
        self.near = [(block, block)]
        for _ in range((depth - 1) // 2):
            above, below = self.near[-1]
            pair = (permute(above, depth, -1), permute(below, depth, 1))
            self.near.append(pair if hold is None else hold(pair))
        self.far = None
        if depth % 2 == 0:
            above, below = self.near[-1]
            half = block.shape[0] // 2
            self.far = (permute(above[:half], depth, -1), permute(below[half:], depth, 1))

    def pieces(self):
        above = [pair[0] for pair in self.near[1:]]
        below = [pair[1] for pair in self.near[:0:-1]]
        return [self.block] + above + list(self.far or ()) + below

    def joined(self, axis, *others):
        near, far = self.near[1:], self.far
        if others:
            near, far, _ = lax.optimization_barrier((near, far, others))
        middle = [] if far is None else [jnp.concatenate(far, axis=0)]
        above = [pair[0] for pair in near]
        below = [pair[1] for pair in near[::-1]]
        return jnp.concatenate([self.block] + above + middle + below, axis=axis)

    def first(self):
        return self.near[-1]

    def last(self):
        return self.near[-1] if self.far is None else self.far


class Scatter:
    def __init__(self, tops, bottoms):
        depth = len(tops)
        self.pairs = [
            [(tops[k], bottoms[-k % depth]) for k in range(depth // 2 + 1)],
            [(bottoms[k], tops[-k % depth]) for k in range((depth - 1) // 2 + 1)],
        ]
        self.depth = depth
        self.first = self.move(self.pairs[0][-1]) if depth > 1 else None

    def move(self, pair):
        return (permute(pair[0], self.depth, 1), permute(pair[1], self.depth, -1))

    def chain(self, pairs, moved):
        for pair in pairs[-2:0:-1]:
            moved = self.move(
                tuple((a.astype(f32) + b.astype(f32)).astype(bf16) for a, b in zip(pair, moved))
            )
        return moved

    def plain(self):
        pairs = self.pairs[1]
        self.second = self.chain(pairs, self.move(pairs[-1])) if len(pairs) > 1 else None
        return self.second

    def added(self, *others):
        pairs = self.pairs[0]
        self.third = self.chain(pairs, after(self.first, *others)) if self.depth > 1 else None
        return self.third

    def total(self, *others):
        top, bottom = self.pairs[0][0]
        top, bottom = top.astype(f32), bottom.astype(f32)
        third, second, _ = lax.optimization_barrier((self.third, self.second, others))
        for pair, swap in ((third, False), (second, True)):
            if pair is not None:
                up, down = pair[::-1] if swap else pair
                top, bottom = top + up.astype(f32), bottom + down.astype(f32)
        return top, bottom


def scatter_straight(blocks):
    depth = len(blocks)
    moved = [permute(blocks[k], depth, k) for k in range(1, depth)]
    return sum((v.astype(f32) for v in moved), blocks[0].astype(f32))


def halves(blocks):
    half = blocks[0].shape[0] // 2
    return [block[:half] for block in blocks], [block[half:] for block in blocks]


def turn_blocks(values, depth, axis, forth=True):
    size = values.shape[axis]
    here = lax.axis_index("z")
    start = (here if forth else (depth - here) % depth) * (size // depth)
    return lax.dynamic_slice_in_dim(
        jnp.concatenate([values, values], axis=axis), start, size, axis
    )


def gather_rows(block):
    return lax.all_gather(block, ROWS, axis=0, tiled=True)


def exchange(values, split, joined, order=ROWS):
    return lax.all_to_all(values, order, split_axis=split, concat_axis=joined, tiled=True)


def split_cores(values, axis=0):
    count = values.shape[axis] // 2
    mine = lax.axis_index("c")
    return [
        lax.dynamic_slice_in_dim(values, core * count, count, axis) for core in (1 - mine, mine)
    ]


def across(values):
    return lax.ppermute(values, "c", [(0, 1), (1, 0)])


def over_chips(total):
    return lax.psum_scatter(total, ("y", "x"), scatter_dimension=0, tiled=True)


def body(
    inputs, cotangent, lengths, w_query, w_key, w_value, w_out, w_gate, w_up, w_down,
    norm_attn, norm_head, norm_ffn, lambda_params, *, depth,
):
    batches, _, rows, width = inputs.shape
    team = H
    chips = team // 2
    shard = w_query.shape[0]
    hidden_shard = w_down.shape[0]
    own_rows = batches * rows
    dims = (2, chips, batches, rows)
    total_rows = 2 * rows
    places = depth * team
    units = depth * hidden_shard
    turned = functools.partial(turn_blocks, depth=depth)

    def natural(blocks):
        shape = blocks.shape
        blocks = blocks.reshape((2, chips, shape[0] // team) + shape[1:])
        return jnp.swapaxes(blocks, 0, 1).reshape(shape)

    def by_core(blocks):
        shape = blocks.shape
        blocks = blocks.reshape((chips, 2, shape[0] // team) + shape[1:])
        return jnp.swapaxes(blocks, 0, 1).reshape(shape)

    x_own = inputs.reshape(own_rows, width)
    x_all = gather_rows(turned(x_own, axis=1))

    qkv = jnp.concatenate(
        [w.reshape(shard, H, 2 * DH) for w in (w_query, w_key, w_value)], axis=2
    )
    qkv = exchange(qkv.transpose(1, 0, 2).reshape(H * shard, 6 * DH), 0, 0)

    small = jnp.concatenate(
        [
            norm_attn.astype(f32), norm_head.astype(f32), norm_ffn.astype(f32),
            lambda_params.astype(f32), lengths[:, 0].astype(f32),
        ]
    )[None]
    small = lax.all_gather(after(small, natural(qkv)), TEAM, axis=0, tiled=True)
    length_all = small[:, -batches:].reshape(chips, 2, batches)[:, 0].astype(jnp.int32)
    far_small = [permute(small, depth, -k) for k in range(1, depth)]
    out_ring = Gather(w_out, depth, lambda near: after(near, natural(qkv)))
    qkv_ring = Gather(
        natural(qkv),
        depth,
        lambda near: after(near, far_small, out_ring.last()),
    )
    small = jnp.concatenate([small] + far_small, axis=0).reshape(depth, team, -1)
    small = turned(small, axis=0, forth=False)
    qkv_near = qkv_ring.first()
    out_w = out_ring.joined(0).reshape(depth, shard, width)
    out_w = lax.all_gather(out_w, TEAM, axis=1, tiled=False)
    out_w = turned(out_w, axis=0, forth=False).reshape(width, width)

    def by_units(w):
        w = w.reshape(shard, depth, team, hidden_shard).transpose(2, 0, 1, 3)
        return w.reshape(team * shard, units)

    gate_up = jnp.concatenate([by_units(w_gate), by_units(w_up)], axis=1)
    n_lam = lambda_params.shape[0]
    gain_attn = small[:, :, :shard].reshape(1, width)
    gain_head = small[:, :, shard : 2 * shard].reshape(H, 2 * DH)
    gain_ffn = small[:, :, 2 * shard : 3 * shard].reshape(1, width)
    lam_parts = small[:, :, 3 * shard : 3 * shard + n_lam].reshape(4, DH)
    first_exp = jnp.exp(jnp.sum(lam_parts[0] * lam_parts[1]))
    second_exp = jnp.exp(jnp.sum(lam_parts[2] * lam_parts[3]))
    lam = (first_exp - second_exp + lambda_init)[None]
    head = lax.axis_index(ROWS)
    gain_mine = lax.dynamic_index_in_dim(gain_head, head, 0) * (1.0 - lambda_init)

    frequency = rope_base ** (-jnp.arange(DH // 2, dtype=f32) / (DH // 2))
    angles = jnp.arange(total_rows, dtype=f32)[:, None] * frequency[None, :]
    cos_table = jnp.concatenate([jnp.cos(angles)] * 2, axis=1)
    sine = jnp.sin(angles)
    sin_table = jnp.concatenate([-sine, sine], axis=1)

    gate_up = exchange(after(gate_up, *qkv_near), 0, 0, TEAM).T
    x_all = after(x_all, *qkv_ring.last(), gate_up)
    inverse_all, normed_one, raw = row_call(
        norm_product_kernel, None, [x_all], [turned(gain_attn, axis=1), qkv_ring.joined(0)], [],
        [(1, f32), (width, bf16), (6 * DH, f32)], [],
    )
    gate_up_ring = Gather(gate_up, depth)
    rot, headed, probs, kept = attend(length_all, lam, raw, cos_table, sin_table, gain_mine, dims)
    headed_own = exchange(headed.reshape(team * own_rows, 2 * DH), 0, 1)
    headed_own = after(headed_own, *gate_up_ring.first())

    x_own = x_own.astype(f32)
    residual = x_own + product(headed_own, out_w)
    inverse_two = inverse_rms(residual)
    unit_two = residual * inverse_two
    normed_two = gather_rows(turned((unit_two * gain_ffn).astype(bf16), axis=1))

    positions = lax.axis_index("c") * rows + jnp.arange(rows, dtype=jnp.int32)
    valid = (positions[None, :] < lengths).reshape(own_rows, 1)
    grad_own = jnp.where(valid, cotangent.reshape(own_rows, width), 0)
    grad_all = gather_rows(grad_own)

    mine = lax.axis_index("c")[None].astype(jnp.int32)
    gate_up_w = gate_up_ring.pieces()
    gate_val, up_val, hidden = row_call(
        gate_up_kernel, None, [normed_two], gate_up_w, [],
        [(units, f32), (units, f32), (units, bf16)], [],
    )
    down_ring = Gather(
        after(w_down, *gate_up_ring.last()), depth, lambda near: after(near, hidden)
    )
    down_w = turned(down_ring.joined(0), axis=0, forth=False)

    (sent,) = row_call(product_kernel, 1 - mine, [hidden], [down_w], [], [], [(width, bf16)])
    (out_rows,) = row_call(
        product_kernel, mine, [hidden], [down_w], [across(sent)], [], [(width, bf16)]
    )
    grad_all = after(grad_all, out_rows)
    out_rows = over_chips(out_rows)

    grads = [(units, bf16), (units, bf16)]
    back_kernel = functools.partial(gate_up_back_kernel, len(gate_up_w))
    back_in = [grad_all, gate_val, up_val]
    *grad_gate_up, sent = row_call(
        back_kernel, 1 - mine, back_in, [down_w, *gate_up_w], [], grads, [(width, bf16)]
    )
    grad_w_down = columns_call(hidden, after(grad_all, sent))
    *grad_gate_up, grad_two = row_call(
        back_kernel, mine, back_in, [down_w, *gate_up_w],
        [after(across(sent), grad_w_down)], grads, [(width, bf16)], grad_gate_up,
    )
    down_blocks = grad_w_down.reshape(depth, hidden_shard, width)
    down_back = Scatter(
        *halves(
            [
                lax.dynamic_index_in_dim(down_blocks, (lax.axis_index("z") + k) % depth, 0, False)
                for k in range(depth)
            ]
        )
    )
    grad_two = after(grad_two, *down_back.first)
    down_back.plain()
    grad_w_gate, grad_w_up = (
        columns_call(after(v, grad_two), normed_two) for v in grad_gate_up
    )
    down_back.added(*down_back.second, grad_w_gate)
    gate_up_back = Scatter(
        *(jnp.split(v, depth, axis=1) for v in (grad_w_gate, grad_w_up))
    )
    gate_up_back.plain()
    gate_up_back.added()
    grad_two = after(
        over_chips(after(grad_two, out_rows)), grad_w_gate, grad_w_up, *gate_up_back.first,
        *down_back.second, *down_back.third,
    )
    grad_two = turned(grad_two, axis=1, forth=False).astype(f32)
    grad_w_down = jnp.concatenate(down_back.total(), axis=0)

    grad_norm_ffn = jnp.sum(grad_two * unit_two, axis=0)
    grad_resid = grad_own.astype(f32) + norm_back(grad_two * gain_ffn, unit_two, inverse_two)
    grad_branch = grad_resid.astype(bf16)
    sent_heads = against(grad_branch, out_w).astype(bf16)
    grad_headed = exchange(sent_heads, 1, 0)
    headed_cores = headed_own.reshape(own_rows, depth, chips, 2, shard).transpose(0, 3, 2, 1, 4)
    headed_cores = turned(headed_cores, axis=3).reshape(own_rows, width)
    theirs, own = split_cores(headed_cores, 1)
    branch = after(grad_branch, sent_heads)
    sent = across(columns_call(theirs, branch))
    grad_w_out = columns_call(own, branch, after(sent, grad_headed))
    grad_headed = after(grad_headed, grad_w_out)
    grad_w_out = over_chips(after(grad_w_out, *gate_up_back.second))
    grad_raw, grad_head, grad_lam = attend_back(
        lam, rot, probs, kept, grad_headed, cos_table, -sin_table, gain_mine, dims
    )
    grad_raw = grad_raw.reshape(team * own_rows, 6 * DH)
    out_rows = after(out_rows, grad_raw)
    output = jnp.where(valid, residual + out_rows.astype(f32), 0.0).astype(bf16)
    qkv_w = qkv_ring.joined(0)
    (sent,) = row_call(against_kernel, 1 - mine, [grad_raw], [qkv_w], [], [], [(width, bf16)])
    sent = after(sent, *gate_up_back.third)
    grad_w_gate_up = jnp.concatenate([v.astype(bf16).T for v in gate_up_back.total()], axis=1)
    grad_w_gate_up = exchange(grad_w_gate_up, 0, 0, TEAM)
    grad_one, norm_sums = row_call(
        inputs_back_kernel, mine, [grad_raw, x_all, inverse_all], [qkv_w],
        [across(sent)], [], [(width, bf16)], sums=[((8, width), f32)],
    )
    grad_norm_attn = turned(jnp.sum(norm_sums, axis=0), axis=0, forth=False)
    grad_one = after(grad_one, grad_w_gate_up)
    grad_qkv = columns_call(normed_one, after(grad_raw, grad_one))
    grad_one = over_chips(grad_one)
    grad_w_out = scatter_straight(jnp.split(grad_w_out, depth, axis=0))
    grad_qkv = after(grad_qkv, grad_w_out)
    qkv_back = Scatter(*halves(jnp.split(grad_qkv, depth, axis=0)))
    grad_w_gate, grad_w_up = place_units(grad_w_gate_up, depth, team)
    qkv_back.plain()
    grad_lam = grad_lam[0, 0]
    grad_lambda = jnp.concatenate(
        [
            grad_lam * first_exp * lam_parts[1],
            grad_lam * first_exp * lam_parts[0],
            -grad_lam * second_exp * lam_parts[3],
            -grad_lam * second_exp * lam_parts[2],
        ]
    )
    grad_head = grad_head * (1.0 - lambda_init)
    head_full = lax.dynamic_update_slice(jnp.zeros((H, 2 * DH), f32), grad_head, (head, 0))
    small_grads = jnp.concatenate(
        [
            grad_norm_attn.reshape(places, shard),
            head_full.reshape(places, shard),
            grad_norm_ffn.reshape(places, shard),
            grad_lambda.reshape(places, n_lam),
        ],
        axis=1,
    )
    small_grads = small_grads.reshape(depth, team, -1).swapaxes(0, 1).reshape(places, -1)
    small_grads = exchange(small_grads, 0, 0, TEAM).reshape(team, depth, -1).sum(axis=0)
    small_grads = lax.all_to_all(small_grads, "z", 0, 0, tiled=True).sum(axis=0)

    qkv_back.added(small_grads)
    grad_qkv = exchange(by_core(jnp.concatenate(qkv_back.total(), axis=0)).astype(bf16), 0, 0)

    inverse_one = inverse_rms(x_own)
    grad_one = after(grad_one, small_grads, grad_w_gate, grad_w_up, grad_w_out)
    grad_one = turned(grad_one, axis=1, forth=False).astype(f32)
    unit_one = x_own * inverse_one
    input_grad = (
        grad_resid + norm_back(grad_one * gain_attn, unit_one, inverse_one)
    ).astype(bf16)

    grad_qkv = place_heads(grad_qkv, 20 * 10**9)

    return (
        output.reshape(inputs.shape),
        input_grad.reshape(inputs.shape),
        grad_qkv[0],
        grad_qkv[1],
        grad_qkv[2],
        grad_w_out,
        grad_w_gate,
        grad_w_up,
        grad_w_down,
        small_grads[:shard],
        small_grads[shard : 2 * shard],
        small_grads[2 * shard : 3 * shard],
        small_grads[3 * shard :],
    )


def solution(mesh):
    cores = mesh.shape["in"]
    depth = mesh.shape["grp"] * cores // H
    split = Mesh(mesh.devices.reshape(depth, 2, H // (2 * cores), cores), EVERY)
    group = ("z", "y", "x")
    data = P(None, group, "c", None)
    matrix = P(EVERY, None)
    vector = P(EVERY)
    return jax.shard_map(
        functools.partial(body, depth=depth),
        mesh=split,
        in_specs=(data, data, P(None, group)) + (matrix,) * 7 + (vector,) * 4,
        out_specs=(data, data) + (matrix,) * 7 + (vector,) * 4,
        check_vma=False,
    )
```
